128 devices in a mesh: fsdp: 32 (over y, x, z_hi), tp: 4 (over z_lo, core).
Axes of the slice: x: 4, y: 4, z: 4 (z_hi: 2, z_lo: 2; z = z_hi * 2 + z_lo), core: 2. Of those that a mesh axis runs over, the one named last changes fastest.
Arguments:
- activations: bfloat16 [65536, 5120], P(('fsdp', 'tp')), may hold values from -24 to 24
- grad_out: bfloat16 [65536, 1024], P(('fsdp', 'tp')), may hold values from -6 to 6
- master_w: float32 [5120, 1024], P(('fsdp', 'tp')), may hold values from -0.078125 to 0.078125
- embed_table: bfloat16 [151936, 5120], P(('fsdp', 'tp')), may hold values from -6 to 6
- token_ids: int32 [256], replicated, may hold values from 0 to 151935
- queries: bfloat16 [256, 8192], P('fsdp', 'tp'), may hold values from -30 to 30
- cache_keys: bfloat16 [256, 512, 1024], P('fsdp', None, 'tp'), may hold values from -6 to 6
- cache_values: bfloat16 [256, 512, 1024], P('fsdp', None, 'tp'), may hold values from -6 to 6
- new_key: bfloat16 [256, 1024], P('fsdp', 'tp'), may hold values from -6 to 6
- first_value: bfloat16 [256, 1024], P('fsdp', 'tp'), may hold values from -6 to 6
- residual_mix: float32 [8], P('tp'), may hold values from 0.2 to 0.8
- lengths: int32 [256], P('fsdp'), may hold values from 1 to 512, 65536 in all
Outputs:
- w_next: float32 [5120, 1024], P(('fsdp', 'tp'))
- new_value: bfloat16 [256, 1024], P('fsdp', 'tp')
- attended: bfloat16 [256, 8192], P('fsdp', 'tp')
The draws below stay inside these ranges and needn't reach their ends.
Inputs may be any that keep to these rules, and one draw needn't show every extreme that they name: `lengths`: some row holds exactly 512 positions.
All inputs are finite; a program needn't handle non-finite values. No bound on the sum of `lengths` on one device may be relied on, other than what follows from the above.
Results may differ from the reference program's by a relative error of at most 0.006.
Values may be sent and summed in bfloat16 or wider, within the bound.
A program may use at most 128 MiB of HBM per device.

```python
import math
import jax
import jax.numpy as jnp
import numpy as np
from jax import lax

D = 5120
HEADS = 64
KV = 8
HD = 128
VOCAB = 151936
TOK_DEV = 512
CTX = 512
KVD = 1024
TOKENS = 65536
ROWS_ALL = 256
DEVICES = 128


def draw_queries(key, part):
    key = jax.random.fold_in(key, 1)
    group = HEADS // KV
    values = jnp.clip(jax.random.normal(key, (ROWS_ALL, KV, group, HD), jnp.float32), -6.0, 6.0)
    return values.reshape(ROWS_ALL, HEADS * HD).astype(jnp.bfloat16)


def draw_cache_keys(key, part):
    key = jax.random.fold_in(key, 2)
    values = jnp.clip(jax.random.normal(key, (ROWS_ALL, CTX, KV, HD), jnp.float32), -6.0, 6.0)
    return values.reshape(ROWS_ALL, CTX, KVD).astype(jnp.bfloat16)


def draw_token_ids(key, part):
    key = jax.random.fold_in(key, 3)
    per_device = ROWS_ALL // DEVICES
    slice_len = VOCAB // DEVICES
    positions = jnp.arange(ROWS_ALL, dtype=jnp.int32)
    home = positions // per_device
    kinds = jax.random.randint(jax.random.fold_in(key, 21), (ROWS_ALL,), 0, 3)
    anywhere = jax.random.randint(jax.random.fold_in(key, 22), (ROWS_ALL,), 0, DEVICES)
    offset = jnp.where(kinds == 0, 1, jnp.where(kinds == 1, DEVICES // 2, anywhere))
    offset = jnp.where(positions % per_device == 0, offset, anywhere)
    owner = (home + offset) % DEVICES
    inside = jax.random.randint(jax.random.fold_in(key, 23), (ROWS_ALL,), 0, slice_len)
    return (owner * slice_len + inside).astype(jnp.int32)


def with_spikes(entries, rng, source, target, shards_of, factor):
    def block_of(dim):
        return (jnp.arange(entries.shape[dim]) // (entries.shape[dim] // shards_of)).reshape((-1,) + (1,) * (entries.ndim - 1 - dim))

    first = jax.random.permutation(rng, shards_of)[block_of(target)]
    far = (block_of(target) + shards_of // 2) % shards_of
    return jnp.where((block_of(source) == first) | (block_of(source) == far), factor * entries, entries)


def level_of(stream_key, shape, split, low, high):
    def one(position, blocks):
        heights = jax.random.uniform(jax.random.fold_in(jax.random.fold_in(stream_key, 6), position), (blocks,), jnp.float32, low / len(split), high / len(split))
        return jnp.repeat(jnp.exp(heights), shape[position] // blocks).reshape((-1,) + (1,) * (len(shape) - position - 1))

    level = one(*split[0])
    for cut in split[1:]:
        level = level * one(*cut)
    return level


def length_profile(count, total, most, lean):
    portions = [(1 << 20) // math.isqrt(grade ** lean) + 1 for grade in range(2, count + 1)]
    surplus, holding = total - most - (count - 1), [1] * (count - 1)
    while surplus > 0:
        free = [i for i in range(count - 1) if holding[i] < most]
        mass, remaining = sum([portions[i] for i in free]), surplus
        for i in free:
            extra = min(most - holding[i], max(1, remaining * portions[i] // mass), surplus)
            holding[i] = holding[i] + extra
            surplus = surplus - extra
    return np.array([most] + holding)


def uneven(own_key, amount, total, bound, lean):
    if amount == 2:
        one = jax.random.randint(own_key, (), max(1, total - bound), min(bound, total - 1) + 1)
        return jnp.stack([one, total - one])
    sizes = jnp.asarray(length_profile(amount, total, bound, lean), jnp.int32)
    couples = (amount - 1) // 2
    giver, sink = sizes[1:1 + 2 * couples:2], sizes[2:2 + 2 * couples:2]
    margin = jnp.minimum(giver - 1, bound - sink)
    shifted = jax.random.randint(jax.random.fold_in(own_key, 1), (couples,), 0, 1 << 20) % (margin + 1)
    sizes = sizes.at[1:1 + 2 * couples:2].set(giver - shifted).at[2:2 + 2 * couples:2].set(sink + shifted)
    return sizes[jax.random.permutation(jax.random.fold_in(own_key, 2), amount)]


def centred(key, extent, deviation, bound, split=(), kind=jnp.bfloat16):
    array = jax.random.normal(key, extent, jnp.float32) * deviation
    if len(split) > 0:
        array = level_of(key, extent, split, -0.22, 0.18) * array
    return jnp.clip(array, min=-bound, max=bound).astype(kind)


def gaussian_with(stream_key, extent, width, reach, cuts, heavy, held_as=jnp.bfloat16):
    values = width * jax.random.normal(stream_key, extent, jnp.float32)
    if cuts:
        values = values * level_of(stream_key, extent, cuts, -0.22, 0.18)
    return jnp.clip(with_spikes(values, jax.random.fold_in(stream_key, 3), *heavy), -reach, reach).astype(held_as)


def setup_inputs(seed: int = 0) -> dict:
    streams_of = jax.random.split(jax.random.key(seed), 13)
    return {
        "activations": gaussian_with(streams_of[0], (TOKENS, D), 1.0, 24.0, ((0, 128),), (0, 1, 128, 5.5)),
        "grad_out": centred(streams_of[1], (TOKENS, KVD), 1.0, 6.0, ((0, 128),)),
        "master_w": centred(streams_of[2], (D, KVD), D ** -0.5, 0.078125, ((0, 128),), jnp.float32),
        "embed_table": centred(streams_of[3], (VOCAB, D), 1.0, 6.0, ((0, 128),)),
        "token_ids": draw_token_ids(jax.random.fold_in(streams_of[12], 71), 0),
        "queries": draw_queries(jax.random.fold_in(streams_of[12], 71), 0),
        "cache_keys": draw_cache_keys(jax.random.fold_in(streams_of[12], 71), 0),
        "cache_values": centred(streams_of[7], (ROWS_ALL, CTX, KVD), 1.0, 6.0, ((0, 32), (2, 4))),
        "new_key": centred(streams_of[8], (ROWS_ALL, KVD), 1.0, 6.0, ((0, 32), (1, 4))),
        "first_value": centred(streams_of[9], (ROWS_ALL, KVD), 1.0, 6.0, ((0, 32), (1, 4))),
        "residual_mix": jnp.clip(0.2 + 0.6 * jax.random.uniform(streams_of[10], (KV,), jnp.float32) ** level_of(streams_of[10], (KV,), ((0, 4),), -0.2, 0.2), 0.2, 0.8),
        "lengths": uneven(streams_of[11], ROWS_ALL, ROWS_ALL * CTX // 2, CTX, 0).astype(jnp.int32),
    }


def reference(activations, grad_out, master_w, embed_table, token_ids, queries, cache_keys, cache_values, new_key, first_value, residual_mix, lengths):
    blocks_a = activations.reshape(DEVICES, TOK_DEV, D)
    blocks_g = grad_out.reshape(DEVICES, TOK_DEV, KVD)

    def accumulate(total, pair):
        left = pair[0].astype(jnp.float32)
        right = pair[1].astype(jnp.float32)
        return (total + jnp.dot(left.T, right), None)
    grad_w, _ = lax.scan(accumulate, jnp.zeros((D, KVD), jnp.float32), (blocks_a, blocks_g))
    coef = 1.0 / math.sqrt(TOKENS * D)
    w_next = master_w - coef * grad_w
    w_roll = w_next.astype(jnp.bfloat16)
    embedded = embed_table[token_ids]
    own_value = jnp.dot(embedded, w_roll, preferred_element_type=jnp.float32)
    share = jnp.repeat(residual_mix, HD)[None, :]
    new_value = (share * own_value + (1.0 - share) * first_value.astype(jnp.float32)).astype(jnp.bfloat16)
    group = HEADS // KV
    scale = 1.0 / math.sqrt(HD)
    query_f = queries.astype(jnp.float32).reshape(ROWS_ALL, KV, group, HD)
    keys_f = cache_keys.astype(jnp.float32).reshape(ROWS_ALL, CTX, KV, HD)
    vals_f = cache_values.astype(jnp.float32).reshape(ROWS_ALL, CTX, KV, HD)
    newk_f = new_key.astype(jnp.float32).reshape(ROWS_ALL, KV, HD)
    newv_f = new_value.astype(jnp.float32).reshape(ROWS_ALL, KV, HD)
    scores = jnp.einsum('rkgd,rckd->rkgc', query_f, keys_f) * scale
    fresh = jnp.einsum('rkgd,rkd->rkg', query_f, newk_f) * scale
    valid = jnp.arange(CTX, dtype=jnp.int32)[None, :] < lengths[:, None]
    scores = jnp.where(valid[:, None, None, :], scores, -1e+30)
    peak = jnp.maximum(lax.optimization_barrier(jnp.max(scores, axis=-1)), fresh)
    expo = jnp.exp(scores - peak[..., None])
    expo_new = jnp.exp(fresh - peak)
    total = lax.optimization_barrier(jnp.sum(expo, axis=-1)) + expo_new
    probs = (expo / total[..., None]).astype(jnp.bfloat16)
    probs_new = (expo_new / total).astype(jnp.bfloat16)
    mixed = jnp.einsum('rkgc,rckd->rkgd', probs.astype(jnp.float32), vals_f)
    mixed = mixed + probs_new.astype(jnp.float32)[..., None] * newv_f[:, :, None, :]
    attended = mixed.reshape(ROWS_ALL, HEADS * HD).astype(jnp.bfloat16)
    return (w_next, new_value, attended)
```

```python
import functools
import math

import jax
import jax.numpy as jnp
from jax import lax
from jax.experimental import pallas as pl
from jax.experimental.pallas import tpu as pltpu
from jax.sharding import PartitionSpec as P

HEADS = 64
KV = 8
HD = 128
MESH = pl.DeviceIdType.MESH
F32 = jnp.float32
BF16 = jnp.bfloat16
RING = 4
STEPS = 8
BLOCK = 640
CHIP_ROWS = 80
ROWS = 40


def order_of(rel):
    return lax.rem(11 - 2 * rel + lax.div(rel, 2), 4)


def distance_at(step):
    return lax.rem(6 - step + 3 * lax.div(step, 2) + 2 * lax.div(step, 3), 4)


def tdot(a, b):
    return lax.dot_general(a, b, (((0,), (0,)), ((), ())), preferred_element_type=F32)


def kernel(
    coef,
    act,
    gout,
    master,
    table,
    tokens,
    first,
    mix,
    w_out,
    value_out,
    act_o,
    act_p,
    gout_o,
    gout_p,
    tab,
    onehot,
    m80,
    w80,
    w_in,
    ex,
    er,
    send,
    recv_p,
    recv_m,
    recv_cp,
    recv_cm,
    send4,
    recv4,
    send2,
    recv2,
    send3,
    recv3,
    emb,
    t1,
    rt1,
    t2,
    rt2,
    t3,
    rt3,
    s_load,
    s_tab,
    s_gm,
    ps_act,
    pr_act,
    ps_gm,
    pr_gm,
    ps_e,
    pr_e,
    ps_x,
    pr_x,
    ss_p,
    sr_p,
    ss_m,
    sr_m,
    ss_cp,
    sr_cp,
    ss_cm,
    sr_cm,
    rs_s,
    rs_r,
    ds_s,
    ds_r,
):
    fsdp = lax.axis_index("fsdp")
    tp = lax.axis_index("tp")
    my_y = lax.div(fsdp, 8)
    my_x = lax.rem(lax.div(fsdp, 2), 4)
    my_z = lax.rem(fsdp, 2) * 2 + lax.div(tp, 2)
    core = lax.rem(tp, 2)
    other = 1 - core

    def device(y, x, z, c):
        return ((y * 4 + x) * 2 + lax.div(z, 2), lax.rem(z, 2) * 2 + c)

    def along(axis, hop):
        y = lax.rem(my_y + hop, 4) if axis == "y" else my_y
        x = lax.rem(my_x + hop, 4) if axis == "x" else my_x
        z = lax.rem(my_z + hop, 4) if axis == "z" else my_z
        return device(y, x, z, core)

    partner = device(my_y, my_x, my_z, other)
    nxt = {a: along(a, 1) for a in "yxz"}
    far = {a: along(a, 2) for a in "yxz"}
    prv = {a: along(a, 3) for a in "yxz"}

    def remote(src, dst, s_sem, r_sem, target):
        return pltpu.make_async_remote_copy(
            src_ref=src,
            dst_ref=dst,
            send_sem=s_sem,
            recv_sem=r_sem,
            device_id=target,
            device_id_type=MESH,
        )

    def columns(i):
        y = lax.rem(my_y + distance_at(lax.div(i, 2)), 4)
        return pl.ds(pl.multiple_of((y * 2 + lax.rem(i, 2)) * BLOCK, 128), BLOCK)

    def quarter(q, c):
        return pl.ds(pl.multiple_of((2 * q + c) * 256, 128), 256)

    def load_act(i):
        return pltpu.make_async_copy(act.at[:, columns(i)], act_o.at[i], s_load.at[i])

    def load_tab(i):
        return pltpu.make_async_copy(table.at[:, columns(i)], tab.at[i], s_tab.at[i])

    def load_gout(q):
        return pltpu.make_async_copy(
            gout.at[:, quarter(q, core)], gout_o.at[:, pl.ds(q * 256, 256)], s_gm.at[q]
        )

    def load_master(q):
        return pltpu.make_async_copy(
            master.at[:, quarter(q, core)], m80.at[core, :, pl.ds(q * 256, 256)], s_gm.at[2 + q]
        )

    def pass_act(i):
        return remote(act.at[:, columns(i)], act_p.at[i], ps_act.at[i], pr_act.at[i], partner)

    def pass_gout(q):
        return remote(
            gout.at[:, quarter(q, other)],
            gout_p.at[:, pl.ds(q * 256, 256)],
            ps_gm.at[q],
            pr_gm.at[q],
            partner,
        )

    def pass_master(q, c):
        return remote(
            master.at[:, quarter(q, 1 - c)],
            m80.at[c, :, pl.ds(q * 256, 256)],
            ps_gm.at[2 + q],
            pr_gm.at[2 + q],
            partner,
        )

    def pass_e(i):
        return remote(ex.at[i], er.at[i], ps_e.at[i], pr_e.at[i], partner)

    for q in range(2):
        load_gout(q).start()

    @pl.loop(0, STEPS)
    def _(i):
        load_tab(i).start()
        load_act(i).start()

    for q in range(2):
        load_master(q).start()

    barrier = pltpu.get_barrier_semaphore()
    peers = [partner] + [d[a] for d in (nxt, far, prv) for a in "yxz"]
    for peer in peers:
        pl.semaphore_signal(barrier, inc=1, device_id=peer, device_id_type=MESH)
    pl.semaphore_wait(barrier, len(peers))

    for q in range(2):
        pass_gout(q).start()

    @pl.loop(0, STEPS)
    def _(i):
        pass_act(i).start()

    for q in range(2):
        pass_master(q, core).start()

    vocab = tab.shape[1]
    start = (fsdp * 4 + tp) * vocab
    row = lax.broadcasted_iota(jnp.int32, (vocab, 128), 0) + start
    onehot[:, 0:128] = (row == tokens[pl.ds(core, 1), :]).astype(F32).astype(BF16)
    onehot[:, 128:256] = (row == tokens[pl.ds(other, 1), :]).astype(F32).astype(BF16)

    axis1 = ("x", "x", "z", "z")

    def plus1(k, s):
        return remote(
            send.at[k, lax.div(s, 2), s],
            recv_p.at[k, s],
            ss_p.at[k, s],
            sr_p.at[k, s],
            nxt[axis1[k]],
        )

    def minus1(k, s):
        return remote(
            send.at[k, 2 - 2 * lax.div(s, 2), s],
            recv_m.at[k, s],
            ss_m.at[k, s],
            sr_m.at[k, s],
            prv[axis1[k]],
        )

    def plus1c(k, s):
        return remote(
            send.at[k, 1, s], recv_cp.at[k, s], ss_cp.at[k, s], sr_cp.at[k, s], nxt[axis1[k]]
        )

    def minus1c(k, s):
        return remote(
            send.at[k, 2, 2 + s], recv_cm.at[k, s], ss_cm.at[k, s], sr_cm.at[k, s], prv[axis1[k]]
        )

    low, high = pl.ds(0, 2), pl.ds(2, 2)

    def ring(buf, into, r, axis):
        def copy(j, place, half, target):
            return remote(
                buf.at[place, half], into.at[j], rs_s.at[r, j], rs_r.at[r, j], target[axis]
            )

        return (
            copy(0, 0, low, nxt),
            copy(1, 1, high, nxt),
            copy(2, 1, low, nxt),
            copy(3, 0, high, prv),
            copy(4, 2, low, prv),
            copy(5, 2, high, prv),
        )

    def ring_pass(buf, into, copies):
        copies[0].wait_recv()
        buf[1, 0:2] = (buf[1, 0:2].astype(F32) + into[0].astype(F32)).astype(BF16)
        copies[2].start()
        copies[3].wait_recv()
        buf[2, 2:4] = (buf[2, 2:4].astype(F32) + into[3].astype(F32)).astype(BF16)
        copies[5].start()

    def ring_sum(buf, into, copies):
        for j in (1, 2, 4, 5):
            copies[j].wait_recv()
        return (
            buf[3, 0:2].astype(F32) + into[2].astype(F32) + into[4].astype(F32),
            buf[3, 2:4].astype(F32) + into[1].astype(F32) + into[5].astype(F32),
        )

    ring4 = ring(send4, recv4, 0, "y")

    @pl.loop(0, STEPS)
    def _(i):
        s = lax.div(i, 2)
        p = lax.rem(i, 2)
        load_tab(i).wait()
        found = tdot(tab[i], onehot[...])
        ex[i] = found[:, 128:256].astype(BF16)
        pass_e(i).start()

        @pl.when(i == 0)
        def _():
            for q in range(2):
                load_gout(q).wait()
                pass_gout(q).wait_recv()

        load_act(i).wait()
        pass_act(i).wait_recv()
        total = tdot(act_o[i], gout_o[...]) + tdot(act_p[i], gout_p[...])
        for b in range(2):
            ox = order_of(lax.rem(2 * p + b + 4 - my_x, 4))
            for z in range(4):
                oz = order_of(lax.rem(z + 4 - my_z, 4))
                rows = slice((b * 4 + z) * CHIP_ROWS, (b * 4 + z + 1) * CHIP_ROWS)
                for k in range(4):
                    part = total[rows, k * 128 : (k + 1) * 128].astype(BF16)
                    if k < 2:
                        send[k, ox, s, oz] = part
                    else:
                        send[k, oz, s, ox] = part
        pass_e(i).wait_recv()
        both = (found[:, 0:128] + er[i].astype(F32)).astype(BF16)
        for b in range(2):
            ox = order_of(lax.rem(2 * p + b + 4 - my_x, 4))
            for z in range(4):
                oz = order_of(lax.rem(z + 4 - my_z, 4))
                rows = slice((b * 4 + z) * CHIP_ROWS, (b * 4 + z + 1) * CHIP_ROWS)
                send4[s, ox, oz] = both[rows, :]

        @pl.when(p == 1)
        def _():
            for k in range(4):
                plus1(k, s).start()
                minus1(k, s).start()

        @pl.when(i == 1)
        def _():
            ring4[0].start()
            ring4[3].start()

        @pl.when(i == 3)
        def _():
            ring4[1].start()

        @pl.when(i == 5)
        def _():
            ring4[4].start()

    ring_pass(send4, recv4, ring4)

    @pl.loop(0, 2)
    def _(s):
        for k in range(4):
            plus1(k, s).wait_recv()
            send[k, 1, s] = (send[k, 1, s].astype(F32) + recv_p[k, s].astype(F32)).astype(BF16)
            plus1c(k, s).start()
            minus1(k, 2 + s).wait_recv()
            send[k, 2, 2 + s] = (
                send[k, 2, 2 + s].astype(F32) + recv_m[k, 2 + s].astype(F32)
            ).astype(BF16)
            minus1c(k, s).start()

    ring2 = [ring(send2.at[k], recv2.at[k], 1 + k, "y" if k < 4 else "x") for k in range(5)]

    def begin2(k):
        for j in (0, 3, 1, 4):
            ring2[k][j].start()

    top, bottom = ring_sum(send4, recv4, ring4)
    send2[4, 0:2] = top.astype(BF16)
    send2[4, 2:4] = bottom.astype(BF16)
    begin2(4)
    for k in range(4):
        for s in range(4):
            if s < 2:
                plus1c(k, s).wait_recv()
                minus1(k, s).wait_recv()
                extra = recv_cp[k, s].astype(F32) + recv_m[k, s].astype(F32)
            else:
                plus1(k, s).wait_recv()
                minus1c(k, s - 2).wait_recv()
                extra = recv_p[k, s].astype(F32) + recv_cm[k, s - 2].astype(F32)
            send2[k, s] = (send[k, 3, s].astype(F32) + extra).astype(BF16)
        begin2(k)
    for k in (4, 0, 1, 2, 3):
        ring_pass(send2.at[k], recv2.at[k], ring2[k])

    def direct(buf, into, r, axis):
        return (
            remote(buf.at[0], into.at[0], ds_s.at[r, 0], ds_r.at[r, 0], far[axis]),
            remote(buf.at[1], into.at[1], ds_s.at[r, 1], ds_r.at[r, 1], nxt[axis]),
            remote(buf.at[2], into.at[2], ds_s.at[r, 2], ds_r.at[r, 2], prv[axis]),
        )

    def direct_sum(buf, into, copies):
        for copy in copies:
            copy.wait_recv()
        return (buf[3].astype(F32) + into[1].astype(F32)) + (
            into[2].astype(F32) + into[0].astype(F32)
        )

    ring3 = [
        direct(send3.at[k], recv3.at[k], k, "x" if k in (2, 3) else "z") for k in range(5)
    ]
    for k in (4, 0, 1, 2, 3):
        top, bottom = ring_sum(send2.at[k], recv2.at[k], ring2[k])
        send3[k, 0:2] = top.astype(BF16)
        send3[k, 2:4] = bottom.astype(BF16)
        for copy in ring3[k]:
            copy.start()

    mine = direct_sum(send3.at[4], recv3.at[4], ring3[4]).astype(BF16)
    emb[core] = mine
    pass_emb = remote(emb.at[core], emb.at[core], ps_x.at[0], pr_x.at[0], partner)
    pass_emb.start()

    for q in range(2):
        load_master(q).wait()
        pass_master(q, other).wait_recv()
    for k in range(4):
        grad = direct_sum(send3.at[k], recv3.at[k], ring3[k])
        span = slice(k * 128, (k + 1) * 128)
        for c in range(2):
            w80[c, :, span] = m80[c, :, span] - coef * grad[c * ROWS : (c + 1) * ROWS]
    pass_w = remote(w80.at[other], w_in, ps_x.at[1], pr_x.at[1], partner)
    pass_w.start()
    for q in range(2):
        w_out[:, quarter(q, core)] = w80[core, :, q * 256 : (q + 1) * 256]
    w_roll = w80[...].reshape(CHIP_ROWS, 512).astype(BF16)

    remote(emb.at[other], emb.at[other], ps_x.at[0], pr_x.at[0], partner).wait_recv()
    oy = [order_of(lax.rem(y + 4 - my_y, 4)) for y in range(4)]
    ox = [order_of(lax.rem(x + 4 - my_x, 4)) for x in range(4)]
    oz = [order_of(lax.rem(z + 4 - my_z, 4)) for z in range(4)]
    for e in range(2):
        part = tdot(emb[e], w_roll)
        for n in range(16):
            block = e * 16 + n
            y, x, z_hi = block // 8, (block // 2) % 4, block % 2
            for z_lo in range(2):
                z = z_hi * 2 + z_lo
                for h in range(2):
                    lane = (z_lo * 2 + h) * 128
                    piece = part[n * 8 : (n + 1) * 8, lane : lane + 128]
                    if h == 0:
                        t1[h, ox[x], oy[y], oz[z]] = piece
                    else:
                        t1[h, oz[z], oy[y], ox[x]] = piece
    tail = (("x", "y", "z"), ("z", "y", "x"))
    sums = []
    stages = ((t1, rt1), (t2, rt2), (t3, rt3))
    tails = [
        [direct(buf.at[h], into.at[h], 5 + 2 * n + h, tail[h][n]) for h in range(2)]
        for n, (buf, into) in enumerate(stages)
    ]
    for n, (buf, into) in enumerate(stages):
        for h in range(2):
            if n > 0:
                before, came = stages[n - 1]
                buf[h] = direct_sum(before.at[h], came.at[h], tails[n - 1][h])
            for copy in tails[n][h]:
                copy.start()
    for h in range(2):
        own = direct_sum(t3.at[h], rt3.at[h], tails[2][h])
        share = mix[h]
        lane = slice(h * 128, (h + 1) * 128)
        value_out[:, lane] = (
            share * own + (1.0 - share) * first[:, lane].astype(F32)
        ).astype(BF16)

    pass_w.wait_recv()
    for q in range(2):
        w_out[:, quarter(q, other)] = w_in[:, q * 256 : (q + 1) * 256]

    @pl.loop(0, STEPS)
    def _(i):
        pass_act(i).wait_send()
        pass_e(i).wait_send()

    for q in range(2):
        pass_gout(q).wait_send()
        pass_master(q, core).wait_send()
    pass_emb.wait_send()
    pass_w.wait_send()

    @pl.loop(0, 4)
    def _(s):
        for k in range(4):
            plus1(k, s).wait_send()
            minus1(k, s).wait_send()

    @pl.loop(0, 2)
    def _(s):
        for k in range(4):
            plus1c(k, s).wait_send()
            minus1c(k, s).wait_send()

    for copies in [ring4] + ring2 + ring3 + tails[0] + tails[1] + tails[2]:
        for copy in copies:
            copy.wait_send()


def update(activations, grad_out, master_w, embed_table, tokens, first_value, mix, tokens_total):
    width = activations.shape[1]
    vocab = embed_table.shape[0]
    depth = activations.shape[0]
    coef = 1.0 / math.sqrt(tokens_total * width)
    dma = pltpu.SemaphoreType.DMA
    vmem = pltpu.VMEM
    tile = (CHIP_ROWS, 128)
    anywhere = pl.BlockSpec(memory_space=pl.ANY)
    whole = pl.BlockSpec(memory_space=pltpu.VMEM)
    return pl.pallas_call(
        functools.partial(kernel, coef),
        out_shape=(
            jax.ShapeDtypeStruct(master_w.shape, F32),
            jax.ShapeDtypeStruct(first_value.shape, BF16),
        ),
        in_specs=[
            anywhere,
            anywhere,
            anywhere,
            anywhere,
            whole,
            whole,
            pl.BlockSpec(memory_space=pltpu.SMEM),
        ],
        out_specs=(whole, whole),
        scratch_shapes=[
            vmem((STEPS, depth, BLOCK), BF16),
            vmem((STEPS, depth, BLOCK), BF16),
            vmem((depth, 512), BF16),
            vmem((depth, 512), BF16),
            vmem((STEPS, vocab, BLOCK), BF16),
            vmem((vocab, 256), BF16),
            vmem((2, ROWS, 512), F32),
            vmem((2, ROWS, 512), F32),
            vmem((ROWS, 512), F32),
            vmem((STEPS, BLOCK, 128), BF16),
            vmem((STEPS, BLOCK, 128), BF16),
            vmem((4, 4, 4, 4) + tile, BF16),
            vmem((4, 4, 4) + tile, BF16),
            vmem((4, 4, 4) + tile, BF16),
            vmem((4, 2, 4) + tile, BF16),
            vmem((4, 2, 4) + tile, BF16),
            vmem((4, 4, 4) + tile, BF16),
            vmem((6, 2, 4) + tile, BF16),
            vmem((5, 4, 4) + tile, BF16),
            vmem((5, 6, 2) + tile, BF16),
            vmem((5, 4) + tile, BF16),
            vmem((5, 3) + tile, BF16),
            vmem((2,) + tile, BF16),
            vmem((2, 4, 4, 4, 8, 128), F32),
            vmem((2, 3, 4, 4, 8, 128), F32),
            vmem((2, 4, 4, 8, 128), F32),
            vmem((2, 3, 4, 8, 128), F32),
            vmem((2, 4, 8, 128), F32),
            vmem((2, 3, 8, 128), F32),
            dma((STEPS,)),
            dma((STEPS,)),
            dma((4,)),
            dma((STEPS,)),
            dma((STEPS,)),
            dma((4,)),
            dma((4,)),
            dma((STEPS,)),
            dma((STEPS,)),
            dma((2,)),
            dma((2,)),
            dma((4, 4)),
            dma((4, 4)),
            dma((4, 4)),
            dma((4, 4)),
            dma((4, 2)),
            dma((4, 2)),
            dma((4, 2)),
            dma((4, 2)),
            dma((6, 6)),
            dma((6, 6)),
            dma((11, 3)),
            dma((11, 3)),
        ],
        compiler_params=pltpu.CompilerParams(
            collective_id=0, has_side_effects=True, vmem_limit_bytes=60 * 1024 * 1024
        ),
        cost_estimate=pl.CostEstimate(
            flops=2 * depth * width * 1024 + 2 * vocab * width * 256,
            bytes_accessed=2 * width * (depth + vocab),
            transcendentals=0,
        ),
        name="update",
    )(activations, grad_out, master_w, embed_table, tokens, first_value, mix)


def per_device(
    activations,
    grad_out,
    master_w,
    embed_table,
    token_ids,
    queries,
    cache_keys,
    cache_values,
    new_key,
    first_value,
    residual_mix,
    lengths,
):
    devices_all = lax.axis_size("fsdp") * lax.axis_size("tp")
    tokens_total = activations.shape[0] * devices_all
    w_next, new_value = update(
        activations,
        grad_out,
        master_w,
        embed_table,
        token_ids.reshape(2, 128),
        first_value,
        residual_mix,
        tokens_total,
    )
    rows = queries.shape[0]
    heads_kv = residual_mix.shape[0]
    group = HEADS // KV
    context = cache_keys.shape[1]
    scale = 1.0 / math.sqrt(HD)
    query_b = queries.reshape(rows, heads_kv, group, HD)
    keys_b = cache_keys.reshape(rows, context, heads_kv, HD)
    vals_b = cache_values.reshape(rows, context, heads_kv, HD)
    newk_b = new_key.reshape(rows, heads_kv, HD)
    newv_b = new_value.reshape(rows, heads_kv, HD)
    scores = (
        jnp.einsum("rkgd,rckd->rkgc", query_b, keys_b, preferred_element_type=jnp.float32) * scale
    )
    fresh = jnp.einsum("rkgd,rkd->rkg", query_b, newk_b, preferred_element_type=jnp.float32) * scale
    valid = jnp.arange(context, dtype=jnp.int32)[None, :] < lengths[:, None]
    scores = jnp.where(valid[:, None, None, :], scores, -1e30)
    peak = jnp.maximum(jnp.max(scores, axis=-1), fresh)
    expo = jnp.exp(scores - peak[..., None])
    expo_new = jnp.exp(fresh - peak)
    total = jnp.sum(expo, axis=-1) + expo_new
    probs = (expo / total[..., None]).astype(jnp.bfloat16)
    probs_new = (expo_new / total).astype(jnp.bfloat16)
    mixed = jnp.einsum("rkgc,rckd->rkgd", probs, vals_b, preferred_element_type=jnp.float32)
    mixed = (
        mixed + probs_new.astype(jnp.float32)[..., None] * newv_b.astype(jnp.float32)[:, :, None, :]
    )
    attended = mixed.reshape(rows, group * heads_kv * HD).astype(jnp.bfloat16)
    return (w_next, new_value, attended)


def solution(mesh):
    return jax.shard_map(
        per_device,
        mesh=mesh,
        in_specs=(
            P(("fsdp", "tp"), None),
            P(("fsdp", "tp"), None),
            P(("fsdp", "tp"), None),
            P(("fsdp", "tp"), None),
            P(),
            P("fsdp", "tp"),
            P("fsdp", None, "tp"),
            P("fsdp", None, "tp"),
            P("fsdp", "tp"),
            P("fsdp", "tp"),
            P("tp"),
            P("fsdp"),
        ),
        out_specs=(P(("fsdp", "tp"), None), P("fsdp", "tp"), P("fsdp", "tp")),
        check_vma=False,
    )
```

```python
import functools
import math

import jax
import jax.numpy as jnp
from jax import lax
from jax.experimental import pallas as pl
from jax.experimental.pallas import tpu as pltpu
from jax.sharding import PartitionSpec as P

HD = 128
MESH = pl.DeviceIdType.MESH
F32 = jnp.float32
BF16 = jnp.bfloat16
STEPS = 8
BLOCK = 640
AHEAD = 2
CHIP_ROWS = 80
ROWS = 40
CUT2 = 48
CUT3 = 64
STACK_A = CHIP_ROWS + CUT3
STACK = CHIP_ROWS + CUT2
EDGE = 2 * CHIP_ROWS - CUT2


def order_of(rel):
    return lax.rem(11 - 2 * rel + lax.div(rel, 2), 4)


def distance_at(step):
    return lax.rem(6 - step + 3 * lax.div(step, 2) + 2 * lax.div(step, 3), 4)


def tdot(a, b):
    return lax.dot_general(a, b, (((0,), (0,)), ((), ())), preferred_element_type=F32)


def kernel(
    coef,
    act,
    gout,
    master,
    table,
    keys,
    vals,
    tokens,
    first,
    query,
    new_key,
    mix,
    lengths,
    w_out,
    value_out,
    att_out,
    act_o,
    act_p,
    gout_o,
    gout_p,
    tab,
    onehot,
    keys_v,
    vals_v,
    qs,
    nk,
    mixed,
    fresh_prob,
    m80,
    w80,
    w_in,
    ex,
    er,
    send_a,
    recv_a,
    send_c,
    recv_c,
    send_b,
    recv_b,
    send2_a,
    send2_c,
    recv2_a,
    recv2_c,
    send2_b,
    recv2_b,
    send3_a,
    send3_c,
    recv3_a,
    recv3_c,
    send3_b,
    recv3_b,
    emb,
    t1,
    t1b,
    rt1,
    t2,
    rt2,
    t3,
    rt3,
    s_load,
    s_tab,
    s_gm,
    s_kv,
    ps_act,
    pr_act,
    ps_gm,
    pr_gm,
    ps_e,
    pr_e,
    ps_x,
    pr_x,
    sa_s,
    sa_r,
    sc_s,
    sc_r,
    sb_s,
    sb_r,
    ds_s,
    ds_r,
):
    fsdp = lax.axis_index("fsdp")
    tp = lax.axis_index("tp")
    my_y = lax.div(fsdp, 8)
    my_x = lax.rem(lax.div(fsdp, 2), 4)
    my_z = lax.rem(fsdp, 2) * 2 + lax.div(tp, 2)
    core = lax.rem(tp, 2)
    other = 1 - core

    def device(y, x, z, c):
        return ((y * 4 + x) * 2 + lax.div(z, 2), lax.rem(z, 2) * 2 + c)

    def along(axis, hop):
        y = lax.rem(my_y + hop, 4) if axis == "y" else my_y
        x = lax.rem(my_x + hop, 4) if axis == "x" else my_x
        z = lax.rem(my_z + hop, 4) if axis == "z" else my_z
        return device(y, x, z, core)

    partner = device(my_y, my_x, my_z, other)
    nxt = {a: along(a, 1) for a in "yxz"}
    far = {a: along(a, 2) for a in "yxz"}
    prv = {a: along(a, 3) for a in "yxz"}
    own_rows = pl.ds(pl.multiple_of(core * ROWS, 8), ROWS)
    other_rows = pl.ds(pl.multiple_of(other * ROWS, 8), ROWS)

    def remote(src, dst, s_sem, r_sem, target):
        return pltpu.make_async_remote_copy(
            src_ref=src,
            dst_ref=dst,
            send_sem=s_sem,
            recv_sem=r_sem,
            device_id=target,
            device_id_type=MESH,
        )

    def pair_at(p):
        return lax.rem(lax.div(my_x, 2) + 1 + p, 2)

    def x_order(w):
        x = 2 * pair_at(w // 2 if isinstance(w, int) else lax.div(w, 2)) + w % 2
        return order_of(lax.rem(x + 4 - my_x, 4))

    def columns(i):
        y = lax.rem(my_y + distance_at(lax.div(i, 2)), 4)
        return pl.ds(pl.multiple_of((y * 2 + pair_at(lax.rem(i, 2))) * BLOCK, 128), BLOCK)

    def quarter(q, c):
        return pl.ds(pl.multiple_of((2 * q + c) * 256, 128), 256)

    def load_act(i):
        return pltpu.make_async_copy(act.at[:, columns(i)], act_o.at[i], s_load.at[i])

    def load_tab(i):
        return pltpu.make_async_copy(table.at[:, columns(i)], tab.at[i], s_tab.at[i])

    def load_gout(q):
        return pltpu.make_async_copy(
            gout.at[:, quarter(q, core)], gout_o.at[:, pl.ds(q * 256, 256)], s_gm.at[q]
        )

    def load_master(q):
        return pltpu.make_async_copy(
            master.at[:, quarter(q, core)],
            m80.at[own_rows, pl.ds(q * 256, 256)],
            s_gm.at[2 + q],
        )

    def pass_act(i):
        return remote(act.at[:, columns(i)], act_p.at[i], ps_act.at[i], pr_act.at[i], partner)

    def pass_gout(q):
        return remote(
            gout.at[:, quarter(q, other)],
            gout_p.at[:, pl.ds(q * 256, 256)],
            ps_gm.at[q],
            pr_gm.at[q],
            partner,
        )

    def pass_master(q, rows):
        return remote(
            master.at[:, quarter(q, other)],
            m80.at[rows, pl.ds(q * 256, 256)],
            ps_gm.at[2 + q],
            pr_gm.at[2 + q],
            partner,
        )

    def pass_e(i):
        return remote(ex.at[i, 1], er.at[i], ps_e.at[i], pr_e.at[i], partner)

    load_tab(0).start()
    for q in range(2):
        load_gout(q).start()

    @pl.loop(0, STEPS - 1)
    def _(i):
        load_act(i).start()
        load_tab(i + 1).start()

    load_act(STEPS - 1).start()

    for q in range(2):
        load_master(q).start()
    load_keys = pltpu.make_async_copy(keys, keys_v, s_kv.at[0])
    load_vals = pltpu.make_async_copy(vals, vals_v, s_kv.at[1])
    load_keys.start()
    load_vals.start()

    barrier = pltpu.get_barrier_semaphore()
    peers = [partner] + [d[a] for d in (nxt, far, prv) for a in "yxz"]
    for peer in peers:
        pl.semaphore_signal(barrier, inc=1, device_id=peer, device_id_type=MESH)
    vocab = tab.shape[1]
    start = (fsdp * 4 + tp) * vocab
    place = (lax.broadcasted_iota(jnp.int32, (128, vocab), 1) + start).astype(F32)
    for e, c in ((0, core), (1, other)):
        named = tokens[:, pl.ds(pl.multiple_of(c * 128, 128), 128)].astype(F32)
        named = jnp.broadcast_to(named, (128, 128)).T[:, 0:1]
        onehot[e * 128 : (e + 1) * 128, :] = (place == named).astype(F32).astype(BF16)
    pl.semaphore_wait(barrier, len(peers))

    for q in range(2):
        pass_gout(q).start()
    for i in range(AHEAD):
        pass_act(i).start()

    places = ((0, 0), (1, 1), (1, 0), (0, 1), (2, 0), (2, 1))

    def copy_a(s, j):
        o, half = places[j]
        return remote(
            send_a.at[o, s, pl.ds(2 * half, 2)],
            recv_a.at[s, j],
            sa_s.at[s, j],
            sa_r.at[s, j],
            nxt["x"] if j < 3 else prv["x"],
        )

    def copy_c(i, j):
        o, half = places[j]
        return remote(
            send_c.at[o, lax.div(i, 2), 2 * lax.rem(i, 2) + half],
            recv_c.at[i, j],
            sc_s.at[i, j],
            sc_r.at[i, j],
            nxt["z"] if j < 3 else prv["z"],
        )

    def copy_b(j):
        o, half = places[j]
        return remote(
            send_b.at[o, pl.ds(2 * half, 2)],
            recv_b.at[j],
            sb_s.at[j],
            sb_r.at[j],
            nxt["y"] if j < 3 else prv["y"],
        )

    def added(x, y):
        return (x.astype(F32) + y.astype(F32)).astype(BF16)

    def forward_a(s):
        copy_a(s, 0).wait_recv()
        send_a[1, s, 0:2] = added(send_a[1, s, 0:2], recv_a[s, 0])
        copy_a(s, 2).start()
        copy_a(s, 3).wait_recv()
        send_a[2, s, 2:4] = added(send_a[2, s, 2:4], recv_a[s, 3])
        copy_a(s, 5).start()

    def forward_c(i):
        st, w = lax.div(i, 2), 2 * lax.rem(i, 2)
        copy_c(i, 0).wait_recv()
        send_c[1, st, w] = added(send_c[1, st, w], recv_c[i, 0])
        copy_c(i, 2).start()
        copy_c(i, 3).wait_recv()
        send_c[2, st, w + 1] = added(send_c[2, st, w + 1], recv_c[i, 3])
        copy_c(i, 5).start()

    def look_up(i):
        load_tab(i).wait()
        found = jnp.dot(onehot[...], tab[i], preferred_element_type=F32)
        ex[i, 0] = found[0:128, :].astype(BF16)
        ex[i, 1] = found[128:256, :].astype(BF16)
        pass_e(i).start()

    look_up(0)
    for q in range(2):
        load_gout(q).wait()
        pass_gout(q).wait_recv()

    @pl.loop(0, STEPS)
    def _(i):
        s = lax.div(i, 2)
        p = lax.rem(i, 2)

        @pl.when(i < STEPS - 1)
        def _():
            look_up(i + 1)

        @pl.when(i + AHEAD < STEPS)
        def _():
            pass_act(i + AHEAD).start()

        load_act(i).wait()
        pass_act(i).wait_recv()
        total = tdot(act_o[i], gout_o[...]) + tdot(act_p[i], gout_p[...])
        for b in range(2):
            w = 2 * p + b
            ox = order_of(lax.rem(2 * pair_at(p) + b + 4 - my_x, 4))
            for z in range(4):
                oz = order_of(lax.rem(z + 4 - my_z, 4))
                part = total[(b * 4 + z) * CHIP_ROWS : (b * 4 + z + 1) * CHIP_ROWS, :].astype(BF16)
                send_a[ox, s, oz, 0:CHIP_ROWS] = part[:, 0:128]
                send_a[ox, s, oz, CHIP_ROWS:STACK_A] = part[0:CUT3, 384:512]
                send_c[oz, s, w, 0:CHIP_ROWS] = part[:, 128:256]
                send_c[oz, s, w, CHIP_ROWS:STACK] = part[0:CUT2, 256:384]
                send_b[s, w, oz, CHIP_ROWS:EDGE] = part[CUT2:, 256:384]
                send_b[s, w, oz, EDGE:STACK] = part[CUT3:, 384:512]
        pass_e(i).wait_recv()
        both = (ex[i, 0].astype(F32) + er[i].astype(F32)).T.astype(BF16)
        for b in range(2):
            w = 2 * p + b
            for z in range(4):
                oz = order_of(lax.rem(z + 4 - my_z, 4))
                send_b[s, w, oz, 0:CHIP_ROWS] = both[
                    (b * 4 + z) * CHIP_ROWS : (b * 4 + z + 1) * CHIP_ROWS, :
                ]

        for j in (0, 3, 1, 4):
            copy_c(i, j).start()

        @pl.when(p == 0)
        def _():
            copy_a(s, 0).start()
            copy_a(s, 3).start()

        @pl.when(p == 1)
        def _():
            copy_a(s, 1).start()
            copy_a(s, 4).start()

        for step, j in ((0, 0), (1, 3), (3, 1), (4, 4)):

            @pl.when(i == step)
            def _(j=j):
                copy_b(j).start()

        @pl.when(i >= 2)
        def _():
            forward_c(i - 2)

        @pl.when((i >= 2) & (p == 0))
        def _():
            forward_a(s - 1)

        @pl.when(i == 5)
        def _():
            copy_b(0).wait_recv()
            send_b[1, 0:2] = added(send_b[1, 0:2], recv_b[0])
            copy_b(2).start()

        @pl.when(i == 7)
        def _():
            copy_b(3).wait_recv()
            send_b[2, 2:4] = added(send_b[2, 2:4], recv_b[3])
            copy_b(5).start()

    forward_c(STEPS - 2)
    forward_a(3)
    forward_c(STEPS - 1)
    for q in range(2):
        pass_master(q, own_rows).start()

    heads = query.shape[1] // HD
    group = heads // 2
    for h in range(heads):
        qs[:, h, :] = query[:, h * HD : (h + 1) * HD].astype(F32)
    for g in range(2):
        nk[:, g, :] = new_key[:, g * HD : (g + 1) * HD].astype(F32)
    load_keys.wait()
    load_vals.wait()
    scale = 1.0 / math.sqrt(HD)
    context = keys.shape[1]
    position = lax.broadcasted_iota(jnp.int32, (group, context), 1)

    def attend(r):
        for g in range(2):
            lanes = slice(g * HD, (g + 1) * HD)
            q = qs[r, g * group : (g + 1) * group, :]
            scores = (
                lax.dot_general(
                    q.astype(BF16),
                    keys_v[r, :, lanes],
                    (((1,), (1,)), ((), ())),
                    preferred_element_type=F32,
                )
                * scale
            )
            fresh = jnp.sum(q * nk[r, g : g + 1, :], axis=1, keepdims=True) * scale
            scores = jnp.where(position < lengths[r], scores, -1e30)
            peak = jnp.maximum(jnp.max(scores, axis=1, keepdims=True), fresh)
            expo = jnp.exp(scores - peak)
            expo_new = jnp.exp(fresh - peak)
            norm = jnp.sum(expo, axis=1, keepdims=True) + expo_new
            probs = (expo / norm).astype(BF16)
            probs_new = (expo_new / norm).astype(BF16).astype(F32)
            mixed[r, g * group : (g + 1) * group, :] = jnp.dot(
                probs, vals_v[r, :, lanes], preferred_element_type=F32
            )
            fresh_prob[r, g * group : (g + 1) * group, :] = jnp.broadcast_to(
                probs_new, (group, HD)
            )

    rows_half = keys.shape[0] // 2
    pl.loop(0, rows_half)(attend)

    def direct(buf, into, r, axis):
        return (
            remote(buf.at[0], into.at[0], ds_s.at[r, 0], ds_r.at[r, 0], far[axis]),
            remote(buf.at[1], into.at[1], ds_s.at[r, 1], ds_r.at[r, 1], nxt[axis]),
            remote(buf.at[2], into.at[2], ds_s.at[r, 2], ds_r.at[r, 2], prv[axis]),
        )

    def direct_sum(buf, into, copies):
        for copy in copies:
            copy.wait_recv()
        return (buf[3].astype(F32) + into[1].astype(F32)) + (
            into[2].astype(F32) + into[0].astype(F32)
        )

    stacks2 = (
        (send2_a, recv2_a, direct(send2_a, recv2_a, 0, "y")),
        (send2_c, recv2_c, direct(send2_c, recv2_c, 1, "x")),
        (send2_b, recv2_b, direct(send2_b, recv2_b, 2, "z")),
    )
    stacks3 = (
        (send3_a, recv3_a, direct(send3_a, recv3_a, 3, "z")),
        (send3_c, recv3_c, direct(send3_c, recv3_c, 4, "y")),
        (send3_b, recv3_b, direct(send3_b, recv3_b, 5, "x")),
    )

    def three(x, y, z):
        return (x.astype(F32) + y.astype(F32) + z.astype(F32)).astype(BF16)

    for j in (1, 2, 4, 5):
        copy_b(j).wait_recv()
    for w in range(4):
        v = w % 2
        came = (recv_b[2, v], recv_b[4, v]) if w < 2 else (recv_b[1, v], recv_b[5, v])
        send2_b[:, x_order(w)] = three(send_b[3, w], *came)
    for copy in stacks2[2][2]:
        copy.start()
    for n in range(4):
        for j in (1, 2, 4, 5):
            copy_a(n, j).wait_recv()
        send2_a[n, 0:2] = three(send_a[3, n, 0:2], recv_a[n, 2], recv_a[n, 4])
        send2_a[n, 2:4] = three(send_a[3, n, 2:4], recv_a[n, 1], recv_a[n, 5])
    for copy in stacks2[0][2]:
        copy.start()
    for n in range(STEPS):
        for j in (1, 2, 4, 5):
            copy_c(n, j).wait_recv()
        st, w = n // 2, 2 * (n % 2)
        send2_c[x_order(w), st] = three(send_c[3, st, w], recv_c[n, 2], recv_c[n, 4])
        send2_c[x_order(w + 1), st] = three(send_c[3, st, w + 1], recv_c[n, 1], recv_c[n, 5])
    for copy in stacks2[1][2]:
        copy.start()
    pl.loop(rows_half, keys.shape[0])(attend)

    for k in (2, 0, 1):
        stacks3[k][0][...] = direct_sum(*stacks2[k]).astype(BF16)
        for copy in stacks3[k][2]:
            copy.start()

    sum_b = direct_sum(*stacks3[2])
    emb[core] = sum_b[0:CHIP_ROWS].astype(BF16)
    pass_emb = remote(emb.at[core], emb.at[core], ps_x.at[0], pr_x.at[0], partner)
    pass_emb.start()

    for q in range(2):
        load_master(q).wait()
        pass_master(q, other_rows).wait_recv()
    sum_a = direct_sum(*stacks3[0])
    w80[:, 0:128] = m80[:, 0:128] - coef * sum_a[0:CHIP_ROWS]
    w80[0:CUT3, 384:512] = m80[0:CUT3, 384:512] - coef * sum_a[CHIP_ROWS:STACK_A]
    w80[CUT3:, 384:512] = m80[CUT3:, 384:512] - coef * sum_b[EDGE:STACK]
    sum_c = direct_sum(*stacks3[1])
    w80[:, 128:256] = m80[:, 128:256] - coef * sum_c[0:CHIP_ROWS]
    w80[0:CUT2, 256:384] = m80[0:CUT2, 256:384] - coef * sum_c[CHIP_ROWS:STACK]
    w80[CUT2:, 256:384] = m80[CUT2:, 256:384] - coef * sum_b[CHIP_ROWS:EDGE]
    pass_w = remote(w80.at[other_rows], w_in, ps_x.at[1], pr_x.at[1], partner)
    pass_w.start()
    w_roll = w80[...].astype(BF16)

    remote(emb.at[other], emb.at[other], ps_x.at[0], pr_x.at[0], partner).wait_recv()
    oy = [order_of(lax.rem(y + 4 - my_y, 4)) for y in range(4)]
    ox = [order_of(lax.rem(x + 4 - my_x, 4)) for x in range(4)]
    oz = [order_of(lax.rem(z + 4 - my_z, 4)) for z in range(4)]
    for e in range(2):
        part = tdot(emb[e], w_roll)
        for n in range(16):
            block = e * 16 + n
            y, x, z_hi = block // 8, (block // 2) % 4, block % 2
            for z_lo in range(2):
                z = z_hi * 2 + z_lo
                for h in range(2):
                    lane = (z_lo * 2 + h) * 128
                    piece = part[n * 8 : (n + 1) * 8, lane : lane + 128]
                    if h == 0:
                        t1[h, ox[x], oy[y], oz[z]] = piece
                    else:
                        t1[h, oz[z], oy[y], ox[x]] = piece
    for h in range(2):
        t1b[h] = t1[h].reshape(4, 4, 2, 16, 128).astype(BF16)
    tail = (("x", "y", "z"), ("z", "y", "x"))
    stages = ((t1b, rt1), (t2, rt2), (t3, rt3))
    tails = [
        [direct(buf.at[h], into.at[h], 6 + 2 * n + h, tail[h][n]) for h in range(2)]
        for n, (buf, into) in enumerate(stages)
    ]
    for n, (buf, into) in enumerate(stages):
        for h in range(2):
            if n > 0:
                before, came = stages[n - 1]
                done = direct_sum(before.at[h], came.at[h], tails[n - 1][h])
                buf[h] = done.reshape(buf.shape[1:])
            for copy in tails[n][h]:
                copy.start()
    for q in range(2):
        w_out[:, quarter(q, core)] = w80[own_rows, q * 256 : (q + 1) * 256]
    pass_w.wait_recv()
    for q in range(2):
        w_out[:, quarter(q, other)] = w_in[:, q * 256 : (q + 1) * 256]
    for h in range(2):
        own = direct_sum(t3.at[h], rt3.at[h], tails[2][h])
        share = mix[h]
        lanes = slice(h * HD, (h + 1) * HD)
        value = (share * own + (1.0 - share) * first[:, lanes].astype(F32)).astype(BF16)
        value_out[:, lanes] = value
        fresh_value = value.astype(F32)
        for n in range(h * group, (h + 1) * group):
            att_out[:, n * HD : (n + 1) * HD] = (
                mixed[:, n, :] + fresh_prob[:, n, :] * fresh_value
            ).astype(BF16)

    @pl.loop(0, STEPS)
    def _(i):
        pass_act(i).wait_send()
        pass_e(i).wait_send()

    for q in range(2):
        pass_gout(q).wait_send()
        pass_master(q, own_rows).wait_send()
    pass_emb.wait_send()
    pass_w.wait_send()

    @pl.loop(0, 4)
    def _(s):
        for j in range(6):
            copy_a(s, j).wait_send()

    @pl.loop(0, STEPS)
    def _(i):
        for j in range(6):
            copy_c(i, j).wait_send()

    for j in range(6):
        copy_b(j).wait_send()
    for _, _, copies in stacks2 + stacks3:
        for copy in copies:
            copy.wait_send()
    for stage in tails:
        for copies in stage:
            for copy in copies:
                copy.wait_send()


def update(
    activations,
    grad_out,
    master_w,
    embed_table,
    cache_keys,
    cache_values,
    tokens,
    first_value,
    queries,
    new_key,
    mix,
    lengths,
    tokens_total,
):
    width = activations.shape[1]
    vocab = embed_table.shape[0]
    depth = activations.shape[0]
    rows = queries.shape[0]
    heads = queries.shape[1] // HD
    coef = 1.0 / math.sqrt(tokens_total * width)
    dma = pltpu.SemaphoreType.DMA
    vmem = pltpu.VMEM
    tile = (STACK, 128)
    tile_a = (STACK_A, 128)
    anywhere = pl.BlockSpec(memory_space=pl.ANY)
    whole = pl.BlockSpec(memory_space=pltpu.VMEM)
    scalars = pl.BlockSpec(memory_space=pltpu.SMEM)
    return pl.pallas_call(
        functools.partial(kernel, coef),
        out_shape=(
            jax.ShapeDtypeStruct(master_w.shape, F32),
            jax.ShapeDtypeStruct(first_value.shape, BF16),
            jax.ShapeDtypeStruct(queries.shape, BF16),
        ),
        in_specs=[anywhere] * 6 + [whole] * 4 + [scalars] * 2,
        out_specs=(whole, whole, whole),
        scratch_shapes=[
            vmem((STEPS, depth, BLOCK), BF16),
            vmem((STEPS, depth, BLOCK), BF16),
            vmem((depth, 512), BF16),
            vmem((depth, 512), BF16),
            vmem((STEPS, vocab, BLOCK), BF16),
            vmem((256, vocab), BF16),
            vmem(cache_keys.shape, BF16),
            vmem(cache_values.shape, BF16),
            vmem((rows, heads, HD), F32),
            vmem((rows, 2, HD), F32),
            vmem((rows, heads, HD), F32),
            vmem((rows, heads, HD), F32),
            vmem((CHIP_ROWS, 512), F32),
            vmem((CHIP_ROWS, 512), F32),
            vmem((ROWS, 512), F32),
            vmem((STEPS, 2, 128, BLOCK), BF16),
            vmem((STEPS, 128, BLOCK), BF16),
            vmem((4, 4, 4) + tile_a, BF16),
            vmem((4, 6, 2) + tile_a, BF16),
            vmem((4, 4, 4) + tile, BF16),
            vmem((STEPS, 6) + tile, BF16),
            vmem((4, 4, 4) + tile, BF16),
            vmem((6, 2, 4) + tile, BF16),
            vmem((4, 4) + tile_a, BF16),
            vmem((4, 4) + tile, BF16),
            vmem((3, 4) + tile_a, BF16),
            vmem((3, 4) + tile, BF16),
            vmem((4, 4) + tile, BF16),
            vmem((3, 4) + tile, BF16),
            vmem((4,) + tile_a, BF16),
            vmem((4,) + tile, BF16),
            vmem((3,) + tile_a, BF16),
            vmem((3,) + tile, BF16),
            vmem((4,) + tile, BF16),
            vmem((3,) + tile, BF16),
            vmem((2, CHIP_ROWS, 128), BF16),
            vmem((2, 4, 4, 4, 8, 128), F32),
            vmem((2, 4, 4, 2, 16, 128), BF16),
            vmem((2, 3, 4, 2, 16, 128), BF16),
            vmem((2, 4, 4, 8, 128), F32),
            vmem((2, 3, 4, 8, 128), F32),
            vmem((2, 4, 8, 128), F32),
            vmem((2, 3, 8, 128), F32),
            dma((STEPS,)),
            dma((STEPS,)),
            dma((4,)),
            dma((2,)),
            dma((STEPS,)),
            dma((STEPS,)),
            dma((4,)),
            dma((4,)),
            dma((STEPS,)),
            dma((STEPS,)),
            dma((2,)),
            dma((2,)),
            dma((4, 6)),
            dma((4, 6)),
            dma((STEPS, 6)),
            dma((STEPS, 6)),
            dma((6,)),
            dma((6,)),
            dma((12, 3)),
            dma((12, 3)),
        ],
        compiler_params=pltpu.CompilerParams(
            collective_id=0, has_side_effects=True, vmem_limit_bytes=60 * 1024 * 1024
        ),
        cost_estimate=pl.CostEstimate(
            flops=2 * depth * width * 1024 + 2 * vocab * width * 256,
            bytes_accessed=2 * width * (depth + vocab),
            transcendentals=0,
        ),
        name="update",
    )(
        activations,
        grad_out,
        master_w,
        embed_table,
        cache_keys,
        cache_values,
        tokens,
        first_value,
        queries,
        new_key,
        mix,
        lengths,
    )


def per_device(
    activations,
    grad_out,
    master_w,
    embed_table,
    token_ids,
    queries,
    cache_keys,
    cache_values,
    new_key,
    first_value,
    residual_mix,
    lengths,
):
    devices_all = lax.axis_size("fsdp") * lax.axis_size("tp")
    return update(
        activations,
        grad_out,
        master_w,
        embed_table,
        cache_keys,
        cache_values,
        token_ids.reshape(1, -1),
        first_value,
        queries,
        new_key,
        residual_mix,
        lengths,
        activations.shape[0] * devices_all,
    )


def solution(mesh):
    return jax.shard_map(
        per_device,
        mesh=mesh,
        in_specs=(
            P(("fsdp", "tp"), None),
            P(("fsdp", "tp"), None),
            P(("fsdp", "tp"), None),
            P(("fsdp", "tp"), None),
            P(),
            P("fsdp", "tp"),
            P("fsdp", None, "tp"),
            P("fsdp", None, "tp"),
            P("fsdp", "tp"),
            P("fsdp", "tp"),
            P("tp"),
            P("fsdp"),
        ),
        out_specs=(P(("fsdp", "tp"), None), P("fsdp", "tp"), P("fsdp", "tp")),
        check_vma=False,
    )
```

```python
import functools
import math

import jax
import jax.numpy as jnp
from jax import lax
from jax.experimental import pallas as pl
from jax.experimental.pallas import tpu as pltpu
from jax.sharding import PartitionSpec as P

HD = 128
MESH = pl.DeviceIdType.MESH
F32 = jnp.float32
BF16 = jnp.bfloat16
STEPS = 8
BLOCK = 640
AHEAD = 2
CHIP_ROWS = 80
ROWS = 40
CUT2 = 64
CUT3 = 64
STACK_A = CHIP_ROWS + CUT3
EDGE = 2 * CHIP_ROWS - CUT2
STACK = EDGE + CHIP_ROWS - CUT3


def order_of(rel):
    return lax.rem(11 - 2 * rel + lax.div(rel, 2), 4)


def distance_at(step):
    return lax.rem(6 - step + 3 * lax.div(step, 2) + 2 * lax.div(step, 3), 4)


def tdot(a, b):
    return lax.dot_general(a, b, (((0,), (0,)), ((), ())), preferred_element_type=F32)


def kernel(
    coef,
    act,
    gout,
    master,
    table,
    keys,
    vals,
    tokens,
    first,
    query,
    new_key,
    mix,
    lengths,
    w_out,
    value_out,
    att_out,
    act_o,
    act_p,
    gout_o,
    gout_p,
    tab,
    onehot,
    keys_v,
    vals_v,
    qs,
    nk,
    mixed,
    fresh_prob,
    m80,
    w80,
    w_in,
    ex,
    er,
    send_a,
    recv_a,
    send_c,
    recv_c,
    send_b,
    recv_b,
    send2_a,
    send2_c,
    recv2_a,
    recv2_c,
    send2_b,
    recv2_b,
    send3_a,
    send3_c,
    recv3_a,
    recv3_c,
    send3_b,
    recv3_b,
    emb,
    t1,
    t1b,
    rt1,
    t2,
    rt2,
    t3,
    rt3,
    s_load,
    s_tab,
    s_gm,
    s_kv,
    ps_act,
    pr_act,
    ps_gm,
    pr_gm,
    ps_e,
    pr_e,
    ps_x,
    pr_x,
    sa_s,
    sa_r,
    sc_s,
    sc_r,
    sb_s,
    sb_r,
    sd_s,
    sd_r,
    ds_s,
    ds_r,
):
    fsdp = lax.axis_index("fsdp")
    tp = lax.axis_index("tp")
    my_y = lax.div(fsdp, 8)
    my_x = lax.rem(lax.div(fsdp, 2), 4)
    my_z = lax.rem(fsdp, 2) * 2 + lax.div(tp, 2)
    core = lax.rem(tp, 2)
    other = 1 - core

    def device(y, x, z, c):
        return ((y * 4 + x) * 2 + lax.div(z, 2), lax.rem(z, 2) * 2 + c)

    def along(axis, hop):
        y = lax.rem(my_y + hop, 4) if axis == "y" else my_y
        x = lax.rem(my_x + hop, 4) if axis == "x" else my_x
        z = lax.rem(my_z + hop, 4) if axis == "z" else my_z
        return device(y, x, z, core)

    partner = device(my_y, my_x, my_z, other)
    nxt = {a: along(a, 1) for a in "yxz"}
    far = {a: along(a, 2) for a in "yxz"}
    prv = {a: along(a, 3) for a in "yxz"}
    own_rows = pl.ds(pl.multiple_of(core * ROWS, 8), ROWS)
    other_rows = pl.ds(pl.multiple_of(other * ROWS, 8), ROWS)

    def remote(src, dst, s_sem, r_sem, target):
        return pltpu.make_async_remote_copy(
            src_ref=src,
            dst_ref=dst,
            send_sem=s_sem,
            recv_sem=r_sem,
            device_id=target,
            device_id_type=MESH,
        )

    def pair_at(p):
        return lax.rem(lax.div(my_x, 2) + 1 + p, 2)

    def x_order(w):
        x = 2 * pair_at(w // 2 if isinstance(w, int) else lax.div(w, 2)) + w % 2
        return order_of(lax.rem(x + 4 - my_x, 4))

    def columns(i):
        y = lax.rem(my_y + distance_at(lax.div(i, 2)), 4)
        return pl.ds(pl.multiple_of((y * 2 + pair_at(lax.rem(i, 2))) * BLOCK, 128), BLOCK)

    def quarter(q, c):
        return pl.ds(pl.multiple_of((2 * q + c) * 256, 128), 256)

    def load_act(i):
        return pltpu.make_async_copy(act.at[:, columns(i)], act_o.at[i], s_load.at[i])

    def load_tab(i):
        return pltpu.make_async_copy(table.at[:, columns(i)], tab.at[i], s_tab.at[i])

    def load_gout(q):
        return pltpu.make_async_copy(
            gout.at[:, quarter(q, core)], gout_o.at[:, pl.ds(q * 256, 256)], s_gm.at[q]
        )

    def load_master(q):
        return pltpu.make_async_copy(
            master.at[:, quarter(q, core)],
            m80.at[own_rows, pl.ds(q * 256, 256)],
            s_gm.at[2 + q],
        )

    def pass_act(i):
        return remote(act.at[:, columns(i)], act_p.at[i], ps_act.at[i], pr_act.at[i], partner)

    def pass_gout(q):
        return remote(
            gout.at[:, quarter(q, other)],
            gout_p.at[:, pl.ds(q * 256, 256)],
            ps_gm.at[q],
            pr_gm.at[q],
            partner,
        )

    def pass_master(q, rows):
        return remote(
            master.at[:, quarter(q, other)],
            m80.at[rows, pl.ds(q * 256, 256)],
            ps_gm.at[2 + q],
            pr_gm.at[2 + q],
            partner,
        )

    def pass_e(i):
        return remote(ex.at[i, 1], er.at[i], ps_e.at[i], pr_e.at[i], partner)

    barrier = pltpu.get_barrier_semaphore()
    peers = [partner] + [d[a] for d in (nxt, far, prv) for a in "yxz"]
    for peer in peers:
        pl.semaphore_signal(barrier, inc=1, device_id=peer, device_id_type=MESH)

    load_tab(0).start()
    for q in range(2):
        load_gout(q).start()

    @pl.loop(0, STEPS - 1)
    def _(i):
        load_act(i).start()
        load_tab(i + 1).start()

    load_act(STEPS - 1).start()

    for q in range(2):
        load_master(q).start()
    load_keys = pltpu.make_async_copy(keys, keys_v, s_kv.at[0])
    load_vals = pltpu.make_async_copy(vals, vals_v, s_kv.at[1])
    load_keys.start()
    load_vals.start()

    vocab = tab.shape[1]
    start = (fsdp * 4 + tp) * vocab
    place = (lax.broadcasted_iota(jnp.int32, (128, vocab), 1) + start).astype(F32)
    for e, c in ((0, core), (1, other)):
        named = tokens[:, pl.ds(pl.multiple_of(c * 128, 128), 128)].astype(F32)
        named = jnp.broadcast_to(named, (128, 128)).T[:, 0:1]
        onehot[e * 128 : (e + 1) * 128, :] = (place == named).astype(F32).astype(BF16)
    pl.semaphore_wait(barrier, len(peers))

    for q in range(2):
        pass_gout(q).start()
    for i in range(AHEAD):
        pass_act(i).start()

    places = ((0, 0), (1, 1), (1, 0), (0, 1), (2, 0), (2, 1))

    def copy_a(s, j):
        o, half = places[j]
        return remote(
            send_a.at[o, s, pl.ds(2 * half, 2)],
            recv_a.at[s, j],
            sa_s.at[s, j],
            sa_r.at[s, j],
            nxt["x"] if j < 3 else prv["x"],
        )

    def copy_c(i, j):
        o, half = places[j]
        return remote(
            send_c.at[o, lax.div(i, 2), 2 * lax.rem(i, 2) + half],
            recv_c.at[i, j],
            sc_s.at[i, j],
            sc_r.at[i, j],
            nxt["z"] if j < 3 else prv["z"],
        )

    def copy_b(j):
        o, half = places[j]
        return remote(
            send_b.at[o, pl.ds(2 * half, 2)],
            recv_b.at[j],
            sb_s.at[j],
            sb_r.at[j],
            nxt["y"] if j < 3 else prv["y"],
        )

    def added(x, y):
        return (x.astype(F32) + y.astype(F32)).astype(BF16)

    def forward_a(s):
        copy_a(s, 0).wait_recv()
        send_a[1, s, 0:2] = added(send_a[1, s, 0:2], recv_a[s, 0])
        copy_a(s, 2).start()
        copy_a(s, 3).wait_recv()
        send_a[2, s, 2:4] = added(send_a[2, s, 2:4], recv_a[s, 3])
        copy_a(s, 5).start()

    def forward_c(i):
        st, w = lax.div(i, 2), 2 * lax.rem(i, 2)
        copy_c(i, 0).wait_recv()
        send_c[1, st, w] = added(send_c[1, st, w], recv_c[i, 0])
        copy_c(i, 2).start()
        copy_c(i, 3).wait_recv()
        send_c[2, st, w + 1] = added(send_c[2, st, w + 1], recv_c[i, 3])
        copy_c(i, 5).start()

    def direct(buf, into, r, axis):
        return (
            remote(buf.at[0], into.at[0], ds_s.at[r, 0], ds_r.at[r, 0], far[axis]),
            remote(buf.at[1], into.at[1], ds_s.at[r, 1], ds_r.at[r, 1], nxt[axis]),
            remote(buf.at[2], into.at[2], ds_s.at[r, 2], ds_r.at[r, 2], prv[axis]),
        )

    def direct_sum(buf, into, copies):
        for copy in copies:
            copy.wait_recv()
        return (buf[3].astype(F32) + into[1].astype(F32)) + (
            into[2].astype(F32) + into[0].astype(F32)
        )

    stacks2 = (
        (send2_a, recv2_a, direct(send2_a, recv2_a, 0, "y")),
        (send2_b, recv2_b, direct(send2_b, recv2_b, 2, "z")),
    )
    stacks3 = (
        (send3_a, recv3_a, direct(send3_a, recv3_a, 3, "z")),
        (send3_c, recv3_c, direct(send3_c, recv3_c, 4, "y")),
        (send3_b, recv3_b, direct(send3_b, recv3_b, 5, "x")),
    )

    pieces = [
        [
            remote(
                send2_c.at[o, n],
                recv2_c.at[o, n],
                sd_s.at[n, o],
                sd_r.at[n, o],
                (far, nxt, prv)[o]["x"],
            )
            for o in range(3)
        ]
        for n in range(4)
    ]

    def three(x, y, z):
        return (x.astype(F32) + y.astype(F32) + z.astype(F32)).astype(BF16)

    def finish_a(n):
        for j in (1, 2, 4, 5):
            copy_a(n, j).wait_recv()
        send2_a[n, 0:2] = three(send_a[3, n, 0:2], recv_a[n, 2], recv_a[n, 4])
        send2_a[n, 2:4] = three(send_a[3, n, 2:4], recv_a[n, 1], recv_a[n, 5])
        if n < 3:
            stacks2[0][2][n].start()

    def finish_c(st):
        for n in (2 * st, 2 * st + 1):
            for j in (1, 2, 4, 5):
                copy_c(n, j).wait_recv()
            w = 2 * (n % 2)
            send2_c[x_order(w), st] = three(send_c[3, st, w], recv_c[n, 2], recv_c[n, 4])
            send2_c[x_order(w + 1), st] = three(send_c[3, st, w + 1], recv_c[n, 1], recv_c[n, 5])
        for copy in pieces[st]:
            copy.start()

    def look_up(i):
        load_tab(i).wait()
        found = jnp.dot(onehot[...], tab[i], preferred_element_type=F32)
        ex[i, 0] = found[0:128, :].astype(BF16)
        ex[i, 1] = found[128:256, :].astype(BF16)
        pass_e(i).start()

    look_up(0)
    for q in range(2):
        load_gout(q).wait()
        pass_gout(q).wait_recv()

    @pl.loop(0, STEPS)
    def _(i):
        s = lax.div(i, 2)
        p = lax.rem(i, 2)

        @pl.when(i + AHEAD < STEPS)
        def _():
            pass_act(i + AHEAD).start()

        load_act(i).wait()
        pass_act(i).wait_recv()
        total = tdot(act_o[i], gout_o[...]) + tdot(act_p[i], gout_p[...])
        for b in range(2):
            w = 2 * p + b
            ox = order_of(lax.rem(2 * pair_at(p) + b + 4 - my_x, 4))
            for z in range(4):
                oz = order_of(lax.rem(z + 4 - my_z, 4))
                part = total[(b * 4 + z) * CHIP_ROWS : (b * 4 + z + 1) * CHIP_ROWS, :].astype(BF16)
                send_a[ox, s, oz, 0:CHIP_ROWS] = part[:, 0:128]
                send_a[ox, s, oz, CHIP_ROWS:STACK_A] = part[0:CUT3, 384:512]
                send_c[oz, s, w, 0:CHIP_ROWS] = part[:, 128:256]
                send_c[oz, s, w, CHIP_ROWS:STACK_A] = part[0:CUT2, 256:384]
                send_b[s, w, oz, CHIP_ROWS:EDGE] = part[CUT2:, 256:384]
                send_b[s, w, oz, EDGE:STACK] = part[CUT3:, 384:512]
        for j in (0, 3, 1, 4):
            copy_c(i, j).start()

        @pl.when(p == 0)
        def _():
            copy_a(s, 0).start()
            copy_a(s, 3).start()

        @pl.when(p == 1)
        def _():
            copy_a(s, 1).start()
            copy_a(s, 4).start()

        pass_e(i).wait_recv()
        both = (ex[i, 0].astype(F32) + er[i].astype(F32)).T.astype(BF16)
        for b in range(2):
            w = 2 * p + b
            for z in range(4):
                oz = order_of(lax.rem(z + 4 - my_z, 4))
                send_b[s, w, oz, 0:CHIP_ROWS] = both[
                    (b * 4 + z) * CHIP_ROWS : (b * 4 + z + 1) * CHIP_ROWS, :
                ]

        for step, j in ((0, 0), (1, 3), (3, 1), (4, 4)):

            @pl.when(i == step)
            def _(j=j):
                copy_b(j).start()

        @pl.when(i < STEPS - 1)
        def _():
            look_up(i + 1)

        @pl.when(i >= 2)
        def _():
            forward_c(i - 2)

        @pl.when((i >= 2) & (p == 0))
        def _():
            forward_a(s - 1)

        @pl.when(i == 4)
        def _():
            copy_b(0).wait_recv()
            send_b[1, 0:2] = added(send_b[1, 0:2], recv_b[0])
            copy_b(2).start()

        @pl.when(i == 6)
        def _():
            copy_b(3).wait_recv()
            send_b[2, 2:4] = added(send_b[2, 2:4], recv_b[3])
            copy_b(5).start()
            finish_a(0)
            finish_c(0)

    forward_c(STEPS - 2)
    forward_a(3)
    forward_c(STEPS - 1)
    for q in range(2):
        pass_master(q, own_rows).start()
    finish_a(1)
    finish_c(1)

    heads = query.shape[1] // HD
    group = heads // 2
    for h in range(heads):
        qs[:, h, :] = query[:, h * HD : (h + 1) * HD].astype(F32)
    for g in range(2):
        nk[:, g, :] = new_key[:, g * HD : (g + 1) * HD].astype(F32)
    load_keys.wait()
    load_vals.wait()
    scale = 1.0 / math.sqrt(HD)
    context = keys.shape[1]
    position = lax.broadcasted_iota(jnp.int32, (group, context), 1)

    def attend(r):
        for g in range(2):
            lanes = slice(g * HD, (g + 1) * HD)
            q = qs[r, g * group : (g + 1) * group, :]
            scores = (
                lax.dot_general(
                    q.astype(BF16),
                    keys_v[r, :, lanes],
                    (((1,), (1,)), ((), ())),
                    preferred_element_type=F32,
                )
                * scale
            )
            fresh = jnp.sum(q * nk[r, g : g + 1, :], axis=1, keepdims=True) * scale
            scores = jnp.where(position < lengths[r], scores, -1e30)
            peak = jnp.maximum(jnp.max(scores, axis=1, keepdims=True), fresh)
            expo = jnp.exp(scores - peak)
            expo_new = jnp.exp(fresh - peak)
            norm = jnp.sum(expo, axis=1, keepdims=True) + expo_new
            probs = (expo / norm).astype(BF16)
            probs_new = (expo_new / norm).astype(BF16).astype(F32)
            mixed[r, g * group : (g + 1) * group, :] = jnp.dot(
                probs, vals_v[r, :, lanes], preferred_element_type=F32
            )
            fresh_prob[r, g * group : (g + 1) * group, :] = jnp.broadcast_to(
                probs_new, (group, HD)
            )

    cuts = [keys.shape[0] * n // 8 for n in (0, 2, 4, 6, 8)]

    finish_a(2)
    finish_c(2)
    for j in (1, 2, 4, 5):
        copy_b(j).wait_recv()
    for w in range(4):
        v = w % 2
        came = (recv_b[2, v], recv_b[4, v]) if w < 2 else (recv_b[1, v], recv_b[5, v])
        send2_b[:, x_order(w)] = three(send_b[3, w], *came)
    for copy in stacks2[1][2]:
        copy.start()
    finish_a(3)
    finish_c(3)
    pl.loop(cuts[0], cuts[1])(attend)

    @pl.loop(0, STEPS)
    def _(i):
        pass_act(i).wait_send()
        pass_e(i).wait_send()
        for j in range(6):
            copy_c(i, j).wait_send()

    @pl.loop(0, 4)
    def _(s):
        for j in range(6):
            copy_a(s, j).wait_send()

    for j in range(6):
        copy_b(j).wait_send()
    for q in range(2):
        pass_gout(q).wait_send()
        pass_master(q, own_rows).wait_send()

    send3_a[...] = direct_sum(*stacks2[0]).astype(BF16)
    for copy in stacks3[0][2]:
        copy.start()
    send3_b[...] = direct_sum(*stacks2[1]).astype(BF16)
    for copy in stacks3[2][2]:
        copy.start()
    for copies in pieces:
        for copy in copies:
            copy.wait_recv()
    send3_c[...] = (
        (send2_c[3].astype(F32) + recv2_c[1].astype(F32))
        + (recv2_c[2].astype(F32) + recv2_c[0].astype(F32))
    ).astype(BF16)
    for copy in stacks3[1][2]:
        copy.start()
    pl.loop(cuts[1], cuts[2])(attend)

    sum_b = direct_sum(*stacks3[2])
    emb[core] = sum_b[0:CHIP_ROWS].astype(BF16)
    pass_emb = remote(emb.at[core], emb.at[core], ps_x.at[0], pr_x.at[0], partner)
    pass_emb.start()

    for q in range(2):
        load_master(q).wait()
        pass_master(q, other_rows).wait_recv()
    sum_a = direct_sum(*stacks3[0])
    w80[:, 0:128] = m80[:, 0:128] - coef * sum_a[0:CHIP_ROWS]
    w80[0:CUT3, 384:512] = m80[0:CUT3, 384:512] - coef * sum_a[CHIP_ROWS:STACK_A]
    w80[CUT3:, 384:512] = m80[CUT3:, 384:512] - coef * sum_b[EDGE:STACK]
    sum_c = direct_sum(*stacks3[1])
    w80[:, 128:256] = m80[:, 128:256] - coef * sum_c[0:CHIP_ROWS]
    w80[0:CUT2, 256:384] = m80[0:CUT2, 256:384] - coef * sum_c[CHIP_ROWS:STACK_A]
    w80[CUT2:, 256:384] = m80[CUT2:, 256:384] - coef * sum_b[CHIP_ROWS:EDGE]
    pass_w = remote(w80.at[other_rows], w_in, ps_x.at[1], pr_x.at[1], partner)
    pass_w.start()
    w_roll = w80[...].astype(BF16)

    remote(emb.at[other], emb.at[other], ps_x.at[0], pr_x.at[0], partner).wait_recv()
    oy = [order_of(lax.rem(y + 4 - my_y, 4)) for y in range(4)]
    ox = [order_of(lax.rem(x + 4 - my_x, 4)) for x in range(4)]
    oz = [order_of(lax.rem(z + 4 - my_z, 4)) for z in range(4)]
    for e in range(2):
        part = tdot(emb[e], w_roll)
        for n in range(16):
            block = e * 16 + n
            y, x, z_hi = block // 8, (block // 2) % 4, block % 2
            for z_lo in range(2):
                z = z_hi * 2 + z_lo
                for h in range(2):
                    lane = (z_lo * 2 + h) * 128
                    piece = part[n * 8 : (n + 1) * 8, lane : lane + 128]
                    if h == 0:
                        t1[h, ox[x], oy[y], oz[z]] = piece
                    else:
                        t1[h, oz[z], oy[y], ox[x]] = piece
    for h in range(2):
        t1b[h] = t1[h].reshape(4, 4, 2, 16, 128).astype(BF16)
    tail = (("x", "y", "z"), ("z", "y", "x"))
    stages = ((t1b, rt1), (t2, rt2), (t3, rt3))
    tails = [
        [direct(buf.at[h], into.at[h], 6 + 2 * n + h, tail[h][n]) for h in range(2)]
        for n, (buf, into) in enumerate(stages)
    ]
    for n, (buf, into) in enumerate(stages):
        for h in range(2):
            if n > 0:
                before, came = stages[n - 1]
                done = direct_sum(before.at[h], came.at[h], tails[n - 1][h])
                buf[h] = done.reshape(buf.shape[1:])
            for copy in tails[n][h]:
                copy.start()
        if n < 2:
            pl.loop(cuts[2 + n], cuts[3 + n])(attend)
    for _, _, copies in stacks2 + stacks3:
        for copy in copies:
            copy.wait_send()
    for copies in pieces:
        for copy in copies:
            copy.wait_send()
    pass_emb.wait_send()
    pass_w.wait_send()
    for q in range(2):
        w_out[:, quarter(q, core)] = w80[own_rows, q * 256 : (q + 1) * 256]
    pass_w.wait_recv()
    for q in range(2):
        w_out[:, quarter(q, other)] = w_in[:, q * 256 : (q + 1) * 256]
    for h in range(2):
        own = direct_sum(t3.at[h], rt3.at[h], tails[2][h])
        share = mix[h]
        lanes = slice(h * HD, (h + 1) * HD)
        value = (share * own + (1.0 - share) * first[:, lanes].astype(F32)).astype(BF16)
        value_out[:, lanes] = value
        fresh_value = value.astype(F32)
        for n in range(h * group, (h + 1) * group):
            att_out[:, n * HD : (n + 1) * HD] = (
                mixed[:, n, :] + fresh_prob[:, n, :] * fresh_value
            ).astype(BF16)

    for stage in tails:
        for copies in stage:
            for copy in copies:
                copy.wait_send()


def update(
    activations,
    grad_out,
    master_w,
    embed_table,
    cache_keys,
    cache_values,
    tokens,
    first_value,
    queries,
    new_key,
    mix,
    lengths,
    tokens_total,
):
    width = activations.shape[1]
    vocab = embed_table.shape[0]
    depth = activations.shape[0]
    rows = queries.shape[0]
    heads = queries.shape[1] // HD
    coef = 1.0 / math.sqrt(tokens_total * width)
    dma = pltpu.SemaphoreType.DMA
    vmem = pltpu.VMEM
    tile = (STACK, 128)
    tile_a = (STACK_A, 128)
    anywhere = pl.BlockSpec(memory_space=pl.ANY)
    whole = pl.BlockSpec(memory_space=pltpu.VMEM)
    scalars = pl.BlockSpec(memory_space=pltpu.SMEM)
    return pl.pallas_call(
        functools.partial(kernel, coef),
        out_shape=(
            vmem(master_w.shape, F32),
            vmem(first_value.shape, BF16),
            vmem(queries.shape, BF16),
        ),
        in_specs=[anywhere] * 6 + [whole] * 4 + [scalars] * 2,
        out_specs=(whole, whole, whole),
        scratch_shapes=[
            vmem((STEPS, depth, BLOCK), BF16),
            vmem((STEPS, depth, BLOCK), BF16),
            vmem((depth, 512), BF16),
            vmem((depth, 512), BF16),
            vmem((STEPS, vocab, BLOCK), BF16),
            vmem((256, vocab), BF16),
            vmem(cache_keys.shape, BF16),
            vmem(cache_values.shape, BF16),
            vmem((rows, heads, HD), F32),
            vmem((rows, 2, HD), F32),
            vmem((rows, heads, HD), F32),
            vmem((rows, heads, HD), F32),
            vmem((CHIP_ROWS, 512), F32),
            vmem((CHIP_ROWS, 512), F32),
            vmem((ROWS, 512), F32),
            vmem((STEPS, 2, 128, BLOCK), BF16),
            vmem((STEPS, 128, BLOCK), BF16),
            vmem((4, 4, 4) + tile_a, BF16),
            vmem((4, 6, 2) + tile_a, BF16),
            vmem((4, 4, 4) + tile_a, BF16),
            vmem((STEPS, 6) + tile_a, BF16),
            vmem((4, 4, 4) + tile, BF16),
            vmem((6, 2, 4) + tile, BF16),
            vmem((4, 4) + tile_a, BF16),
            vmem((4, 4) + tile_a, BF16),
            vmem((3, 4) + tile_a, BF16),
            vmem((3, 4) + tile_a, BF16),
            vmem((4, 4) + tile, BF16),
            vmem((3, 4) + tile, BF16),
            vmem((4,) + tile_a, BF16),
            vmem((4,) + tile_a, BF16),
            vmem((3,) + tile_a, BF16),
            vmem((3,) + tile_a, BF16),
            vmem((4,) + tile, BF16),
            vmem((3,) + tile, BF16),
            vmem((2, CHIP_ROWS, 128), BF16),
            vmem((2, 4, 4, 4, 8, 128), F32),
            vmem((2, 4, 4, 2, 16, 128), BF16),
            vmem((2, 3, 4, 2, 16, 128), BF16),
            vmem((2, 4, 4, 8, 128), F32),
            vmem((2, 3, 4, 8, 128), F32),
            vmem((2, 4, 8, 128), F32),
            vmem((2, 3, 8, 128), F32),
            dma((STEPS,)),
            dma((STEPS,)),
            dma((4,)),
            dma((2,)),
            dma((STEPS,)),
            dma((STEPS,)),
            dma((4,)),
            dma((4,)),
            dma((STEPS,)),
            dma((STEPS,)),
            dma((2,)),
            dma((2,)),
            dma((4, 6)),
            dma((4, 6)),
            dma((STEPS, 6)),
            dma((STEPS, 6)),
            dma((6,)),
            dma((6,)),
            dma((4, 3)),
            dma((4, 3)),
            dma((12, 3)),
            dma((12, 3)),
        ],
        compiler_params=pltpu.CompilerParams(
            collective_id=0, has_side_effects=True, vmem_limit_bytes=60 * 1024 * 1024
        ),
        cost_estimate=pl.CostEstimate(
            flops=2 * depth * width * 1024 + 2 * vocab * width * 256,
            bytes_accessed=2 * width * (depth + vocab),
            transcendentals=0,
        ),
        name="update",
    )(
        activations,
        grad_out,
        master_w,
        embed_table,
        cache_keys,
        cache_values,
        tokens,
        first_value,
        queries,
        new_key,
        mix,
        lengths,
    )


def per_device(
    activations,
    grad_out,
    master_w,
    embed_table,
    token_ids,
    queries,
    cache_keys,
    cache_values,
    new_key,
    first_value,
    residual_mix,
    lengths,
):
    devices_all = lax.axis_size("fsdp") * lax.axis_size("tp")
    return update(
        activations,
        grad_out,
        master_w,
        embed_table,
        cache_keys,
        cache_values,
        token_ids.reshape(1, -1),
        first_value,
        queries,
        new_key,
        residual_mix,
        lengths,
        activations.shape[0] * devices_all,
    )


def solution(mesh):
    return jax.shard_map(
        per_device,
        mesh=mesh,
        in_specs=(
            P(("fsdp", "tp"), None),
            P(("fsdp", "tp"), None),
            P(("fsdp", "tp"), None),
            P(("fsdp", "tp"), None),
            P(),
            P("fsdp", "tp"),
            P("fsdp", None, "tp"),
            P("fsdp", None, "tp"),
            P("fsdp", "tp"),
            P("fsdp", "tp"),
            P("tp"),
            P("fsdp"),
        ),
        out_specs=(P(("fsdp", "tp"), None), P("fsdp", "tp"), P("fsdp", "tp")),
        check_vma=False,
    )
```

```python
import functools
import math

import jax
import jax.numpy as jnp
from jax import lax
from jax.experimental import pallas as pl
from jax.experimental.pallas import tpu as pltpu
from jax.sharding import PartitionSpec as P

HD = 128
MESH = pl.DeviceIdType.MESH
F32 = jnp.float32
BF16 = jnp.bfloat16
STEPS = 8
BLOCK = 640
AHEAD = 2
CHIP_ROWS = 80
ROWS = 40
CUT2 = 64
CUT3 = 64
STACK_A = CHIP_ROWS + CUT3
EDGE = 2 * CHIP_ROWS - CUT2
STACK = EDGE + CHIP_ROWS - CUT3


def order_of(rel):
    return lax.rem(11 - 2 * rel + lax.div(rel, 2), 4)


def distance_at(step):
    return lax.rem(6 - step + 3 * lax.div(step, 2) + 2 * lax.div(step, 3), 4)


def tdot(a, b):
    return lax.dot_general(a, b, (((0,), (0,)), ((), ())), preferred_element_type=F32)


def kernel(
    coef,
    act,
    gout,
    master,
    table,
    keys,
    vals,
    tokens,
    first,
    query,
    new_key,
    mix,
    lengths,
    w_out,
    value_out,
    att_out,
    act_o,
    act_p,
    gout_o,
    gout_p,
    tab,
    onehot,
    keys_v,
    vals_v,
    qs,
    nk,
    mixed,
    fresh_prob,
    m80,
    w80,
    w_in,
    ex,
    er,
    send_a,
    recv_a,
    send_c,
    recv_c,
    send_b,
    recv_b,
    send2_a,
    send2_c,
    recv2_a,
    recv2_c,
    send2_b,
    recv2_b,
    send3_a,
    send3_c,
    recv3_a,
    recv3_c,
    send3_b,
    recv3_b,
    emb,
    t1,
    t1b,
    rt1,
    t2,
    rt2,
    t3,
    rt3,
    s_load,
    s_tab,
    s_gm,
    s_kv,
    ps_act,
    pr_act,
    ps_gm,
    pr_gm,
    ps_e,
    pr_e,
    ps_x,
    pr_x,
    sa_s,
    sa_r,
    sc_s,
    sc_r,
    sb_s,
    sb_r,
    sd_s,
    sd_r,
    ds_s,
    ds_r,
):
    fsdp = lax.axis_index("fsdp")
    tp = lax.axis_index("tp")
    my_y = lax.div(fsdp, 8)
    my_x = lax.rem(lax.div(fsdp, 2), 4)
    my_z = lax.rem(fsdp, 2) * 2 + lax.div(tp, 2)
    core = lax.rem(tp, 2)
    other = 1 - core

    def device(y, x, z, c):
        return ((y * 4 + x) * 2 + lax.div(z, 2), lax.rem(z, 2) * 2 + c)

    def along(axis, hop):
        y = lax.rem(my_y + hop, 4) if axis == "y" else my_y
        x = lax.rem(my_x + hop, 4) if axis == "x" else my_x
        z = lax.rem(my_z + hop, 4) if axis == "z" else my_z
        return device(y, x, z, core)

    partner = device(my_y, my_x, my_z, other)
    nxt = {a: along(a, 1) for a in "yxz"}
    far = {a: along(a, 2) for a in "yxz"}
    prv = {a: along(a, 3) for a in "yxz"}
    own_rows = pl.ds(pl.multiple_of(core * ROWS, 8), ROWS)
    other_rows = pl.ds(pl.multiple_of(other * ROWS, 8), ROWS)

    def remote(src, dst, s_sem, r_sem, target):
        return pltpu.make_async_remote_copy(
            src_ref=src,
            dst_ref=dst,
            send_sem=s_sem,
            recv_sem=r_sem,
            device_id=target,
            device_id_type=MESH,
        )

    def pair_at(p):
        return lax.rem(lax.div(my_x, 2) + 1 + p, 2)

    def x_order(w):
        x = 2 * pair_at(w // 2 if isinstance(w, int) else lax.div(w, 2)) + w % 2
        return order_of(lax.rem(x + 4 - my_x, 4))

    def columns(i):
        y = lax.rem(my_y + distance_at(lax.div(i, 2)), 4)
        return pl.ds(pl.multiple_of((y * 2 + pair_at(lax.rem(i, 2))) * BLOCK, 128), BLOCK)

    def quarter(q, c):
        return pl.ds(pl.multiple_of((2 * q + c) * 256, 128), 256)

    def load_act(i):
        return pltpu.make_async_copy(act.at[:, columns(i)], act_o.at[i], s_load.at[i])

    def load_tab(i):
        return pltpu.make_async_copy(table.at[:, columns(i)], tab.at[i], s_tab.at[i])

    def load_gout(q):
        return pltpu.make_async_copy(
            gout.at[:, quarter(q, core)], gout_o.at[:, pl.ds(q * 256, 256)], s_gm.at[q]
        )

    def load_master(q):
        return pltpu.make_async_copy(
            master.at[:, quarter(q, core)],
            m80.at[own_rows, pl.ds(q * 256, 256)],
            s_gm.at[2 + q],
        )

    def pass_act(i):
        return remote(act.at[:, columns(i)], act_p.at[i], ps_act.at[i], pr_act.at[i], partner)

    def pass_gout(q):
        return remote(
            gout.at[:, quarter(q, other)],
            gout_p.at[:, pl.ds(q * 256, 256)],
            ps_gm.at[q],
            pr_gm.at[q],
            partner,
        )

    def pass_master(q, rows):
        return remote(
            master.at[:, quarter(q, other)],
            m80.at[rows, pl.ds(q * 256, 256)],
            ps_gm.at[2 + q],
            pr_gm.at[2 + q],
            partner,
        )

    def pass_e(i):
        return remote(ex.at[i, 1], er.at[i], ps_e.at[i], pr_e.at[i], partner)

    barrier = pltpu.get_barrier_semaphore()
    peers = [partner] + [d[a] for d in (nxt, far, prv) for a in "yxz"]
    for peer in peers:
        pl.semaphore_signal(barrier, inc=1, device_id=peer, device_id_type=MESH)

    load_tab(0).start()
    for q in range(2):
        load_gout(q).start()

    @pl.loop(0, STEPS - 1)
    def _(i):
        load_act(i).start()
        load_tab(i + 1).start()

    load_act(STEPS - 1).start()

    for q in range(2):
        load_master(q).start()
    load_keys = pltpu.make_async_copy(keys, keys_v, s_kv.at[0])
    load_vals = pltpu.make_async_copy(vals, vals_v, s_kv.at[1])
    load_keys.start()
    load_vals.start()

    vocab = tab.shape[1]
    start = (fsdp * 4 + tp) * vocab
    place = (lax.broadcasted_iota(jnp.int32, (128, vocab), 1) + start).astype(F32)
    for e, c in ((0, core), (1, other)):
        named = tokens[:, pl.ds(pl.multiple_of(c * 128, 128), 128)].astype(F32)
        named = jnp.broadcast_to(named, (128, 128)).T[:, 0:1]
        onehot[e * 128 : (e + 1) * 128, :] = (place == named).astype(F32).astype(BF16)
    pl.semaphore_wait(barrier, len(peers))

    for q in range(2):
        pass_gout(q).start()
    for i in range(AHEAD):
        pass_act(i).start()

    places = ((0, 0), (1, 1), (1, 0), (0, 1), (2, 0), (2, 1))

    def copy_a(s, j):
        o, half = places[j]
        return remote(
            send_a.at[o, s, pl.ds(2 * half, 2)],
            recv_a.at[s, j],
            sa_s.at[s, j],
            sa_r.at[s, j],
            nxt["x"] if j < 3 else prv["x"],
        )

    def copy_c(i, j):
        o, half = places[j]
        return remote(
            send_c.at[o, lax.div(i, 2), 2 * lax.rem(i, 2) + half],
            recv_c.at[i, j],
            sc_s.at[i, j],
            sc_r.at[i, j],
            nxt["z"] if j < 3 else prv["z"],
        )

    def copy_b(j):
        o, half = places[j]
        return remote(
            send_b.at[o, pl.ds(2 * half, 2)],
            recv_b.at[j],
            sb_s.at[j],
            sb_r.at[j],
            nxt["y"] if j < 3 else prv["y"],
        )

    def added(x, y):
        return (x.astype(F32) + y.astype(F32)).astype(BF16)

    def forward_a(s):
        copy_a(s, 0).wait_recv()
        send_a[1, s, 0:2] = added(send_a[1, s, 0:2], recv_a[s, 0])
        copy_a(s, 2).start()
        copy_a(s, 3).wait_recv()
        send_a[2, s, 2:4] = added(send_a[2, s, 2:4], recv_a[s, 3])
        copy_a(s, 5).start()

    def forward_c(i):
        st, w = lax.div(i, 2), 2 * lax.rem(i, 2)
        copy_c(i, 0).wait_recv()
        send_c[1, st, w] = added(send_c[1, st, w], recv_c[i, 0])
        copy_c(i, 2).start()
        copy_c(i, 3).wait_recv()
        send_c[2, st, w + 1] = added(send_c[2, st, w + 1], recv_c[i, 3])
        copy_c(i, 5).start()

    def direct(buf, into, r, axis):
        return (
            remote(buf.at[0], into.at[0], ds_s.at[r, 0], ds_r.at[r, 0], far[axis]),
            remote(buf.at[1], into.at[1], ds_s.at[r, 1], ds_r.at[r, 1], nxt[axis]),
            remote(buf.at[2], into.at[2], ds_s.at[r, 2], ds_r.at[r, 2], prv[axis]),
        )

    def direct_sum(buf, into, copies):
        for copy in copies:
            copy.wait_recv()
        return (buf[3].astype(F32) + into[1].astype(F32)) + (
            into[2].astype(F32) + into[0].astype(F32)
        )

    stacks2 = (
        (send2_a, recv2_a, direct(send2_a, recv2_a, 0, "y")),
        (send2_b, recv2_b, direct(send2_b, recv2_b, 2, "z")),
    )
    stacks3 = (
        (send3_a, recv3_a, direct(send3_a, recv3_a, 3, "z")),
        (send3_c, recv3_c, direct(send3_c, recv3_c, 4, "y")),
        (send3_b, recv3_b, direct(send3_b, recv3_b, 5, "x")),
    )

    pieces = [
        [
            remote(
                send2_c.at[o, n],
                recv2_c.at[o, n],
                sd_s.at[n, o],
                sd_r.at[n, o],
                (far, nxt, prv)[o]["x"],
            )
            for o in range(3)
        ]
        for n in range(4)
    ]

    def three(x, y, z):
        return (x.astype(F32) + y.astype(F32) + z.astype(F32)).astype(BF16)

    def finish_a(n):
        for j in (1, 2, 4, 5):
            copy_a(n, j).wait_recv()
        send2_a[n, 0:2] = three(send_a[3, n, 0:2], recv_a[n, 2], recv_a[n, 4])
        send2_a[n, 2:4] = three(send_a[3, n, 2:4], recv_a[n, 1], recv_a[n, 5])
        if n < 3:
            stacks2[0][2][n].start()

    def finish_c(st):
        for n in (2 * st, 2 * st + 1):
            for j in (1, 2, 4, 5):
                copy_c(n, j).wait_recv()
            w = 2 * (n % 2)
            send2_c[x_order(w), st] = three(send_c[3, st, w], recv_c[n, 2], recv_c[n, 4])
            send2_c[x_order(w + 1), st] = three(send_c[3, st, w + 1], recv_c[n, 1], recv_c[n, 5])
        for copy in pieces[st]:
            copy.start()

    def look_up(i):
        load_tab(i).wait()
        found = jnp.dot(onehot[...], tab[i], preferred_element_type=F32)
        ex[i, 0] = found[0:128, :].astype(BF16)
        ex[i, 1] = found[128:256, :].astype(BF16)
        pass_e(i).start()

    look_up(0)
    for q in range(2):
        load_gout(q).wait()
        pass_gout(q).wait_recv()

    @pl.loop(0, STEPS)
    def _(i):
        s = lax.div(i, 2)
        p = lax.rem(i, 2)

        @pl.when(i + AHEAD < STEPS)
        def _():
            pass_act(i + AHEAD).start()

        load_act(i).wait()
        pass_act(i).wait_recv()
        total = tdot(act_o[i], gout_o[...]) + tdot(act_p[i], gout_p[...])
        for b in range(2):
            w = 2 * p + b
            ox = order_of(lax.rem(2 * pair_at(p) + b + 4 - my_x, 4))
            for z in range(4):
                oz = order_of(lax.rem(z + 4 - my_z, 4))
                part = total[(b * 4 + z) * CHIP_ROWS : (b * 4 + z + 1) * CHIP_ROWS, :].astype(BF16)
                send_a[ox, s, oz, 0:CHIP_ROWS] = part[:, 0:128]
                send_a[ox, s, oz, CHIP_ROWS:STACK_A] = part[0:CUT3, 384:512]
                send_c[oz, s, w, 0:CHIP_ROWS] = part[:, 128:256]
                send_c[oz, s, w, CHIP_ROWS:STACK_A] = part[0:CUT2, 256:384]
                send_b[s, w, oz, CHIP_ROWS:EDGE] = part[CUT2:, 256:384]
                send_b[s, w, oz, EDGE:STACK] = part[CUT3:, 384:512]
        for j in (0, 3, 1, 4):
            copy_c(i, j).start()

        @pl.when(p == 0)
        def _():
            copy_a(s, 0).start()
            copy_a(s, 3).start()

        @pl.when(p == 1)
        def _():
            copy_a(s, 1).start()
            copy_a(s, 4).start()

        pass_e(i).wait_recv()
        both = (ex[i, 0].astype(F32) + er[i].astype(F32)).T.astype(BF16)
        for b in range(2):
            w = 2 * p + b
            for z in range(4):
                oz = order_of(lax.rem(z + 4 - my_z, 4))
                send_b[s, w, oz, 0:CHIP_ROWS] = both[
                    (b * 4 + z) * CHIP_ROWS : (b * 4 + z + 1) * CHIP_ROWS, :
                ]

        for step, j in ((0, 0), (1, 3), (3, 1), (4, 4)):

            @pl.when(i == step)
            def _(j=j):
                copy_b(j).start()

        @pl.when(i < STEPS - 1)
        def _():
            look_up(i + 1)

        @pl.when(i >= 2)
        def _():
            forward_c(i - 2)

        @pl.when((i >= 2) & (p == 0))
        def _():
            forward_a(s - 1)

        @pl.when(i == 4)
        def _():
            copy_b(0).wait_recv()
            send_b[1, 0:2] = added(send_b[1, 0:2], recv_b[0])
            copy_b(2).start()

        @pl.when(i == 6)
        def _():
            copy_b(3).wait_recv()
            send_b[2, 2:4] = added(send_b[2, 2:4], recv_b[3])
            copy_b(5).start()
            finish_a(0)
            finish_c(0)

    forward_c(STEPS - 2)
    forward_a(3)
    forward_c(STEPS - 1)
    for q in range(2):
        pass_master(q, own_rows).start()
    finish_a(1)
    finish_c(1)

    heads = query.shape[1] // HD
    group = heads // 2
    for h in range(heads):
        qs[:, h, :] = query[:, h * HD : (h + 1) * HD].astype(F32)
    for g in range(2):
        nk[:, g, :] = new_key[:, g * HD : (g + 1) * HD].astype(F32)
    load_keys.wait()
    load_vals.wait()
    scale = 1.0 / math.sqrt(HD)
    context = keys.shape[1]
    position = lax.broadcasted_iota(jnp.int32, (group, context), 1)

    def attend(r):
        for g in range(2):
            lanes = slice(g * HD, (g + 1) * HD)
            q = qs[r, g * group : (g + 1) * group, :]
            scores = (
                lax.dot_general(
                    q.astype(BF16),
                    keys_v[r, :, lanes],
                    (((1,), (1,)), ((), ())),
                    preferred_element_type=F32,
                )
                * scale
            )
            fresh = jnp.sum(q * nk[r, g : g + 1, :], axis=1, keepdims=True) * scale
            scores = jnp.where(position < lengths[r], scores, -1e30)
            peak = jnp.maximum(jnp.max(scores, axis=1, keepdims=True), fresh)
            expo = jnp.exp(scores - peak)
            expo_new = jnp.exp(fresh - peak)
            norm = jnp.sum(expo, axis=1, keepdims=True) + expo_new
            probs = (expo / norm).astype(BF16)
            probs_new = (expo_new / norm).astype(BF16).astype(F32)
            mixed[r, g * group : (g + 1) * group, :] = jnp.dot(
                probs, vals_v[r, :, lanes], preferred_element_type=F32
            )
            fresh_prob[r, g * group : (g + 1) * group, :] = jnp.broadcast_to(
                probs_new, (group, HD)
            )

    cuts = [keys.shape[0] * n // 8 for n in (0, 2, 4, 6, 8)]

    finish_a(2)
    for j in (1, 2, 4, 5):
        copy_b(j).wait_recv()
    for w in range(4):
        v = w % 2
        came = (recv_b[2, v], recv_b[4, v]) if w < 2 else (recv_b[1, v], recv_b[5, v])
        send2_b[:, x_order(w)] = three(send_b[3, w], *came)
    for copy in stacks2[1][2]:
        copy.start()
    finish_c(2)
    finish_a(3)
    finish_c(3)
    pl.loop(cuts[0], cuts[1])(attend)

    @pl.loop(0, STEPS)
    def _(i):
        pass_act(i).wait_send()
        pass_e(i).wait_send()
        for j in range(6):
            copy_c(i, j).wait_send()

    @pl.loop(0, 4)
    def _(s):
        for j in range(6):
            copy_a(s, j).wait_send()

    for j in range(6):
        copy_b(j).wait_send()
    for q in range(2):
        pass_gout(q).wait_send()
        pass_master(q, own_rows).wait_send()

    send3_b[...] = direct_sum(*stacks2[1]).astype(BF16)
    for copy in stacks3[2][2]:
        copy.start()
    send3_a[...] = direct_sum(*stacks2[0]).astype(BF16)
    for copy in stacks3[0][2]:
        copy.start()
    for copies in pieces:
        for copy in copies:
            copy.wait_recv()
    send3_c[...] = (
        (send2_c[3].astype(F32) + recv2_c[1].astype(F32))
        + (recv2_c[2].astype(F32) + recv2_c[0].astype(F32))
    ).astype(BF16)
    for copy in stacks3[1][2]:
        copy.start()
    pl.loop(cuts[1], cuts[2])(attend)

    sum_b = direct_sum(*stacks3[2])
    emb[core] = sum_b[0:CHIP_ROWS].astype(BF16)
    pass_emb = remote(emb.at[core], emb.at[core], ps_x.at[0], pr_x.at[0], partner)
    pass_emb.start()

    for q in range(2):
        load_master(q).wait()
        pass_master(q, other_rows).wait_recv()
    sum_a = direct_sum(*stacks3[0])
    w80[:, 0:128] = m80[:, 0:128] - coef * sum_a[0:CHIP_ROWS]
    w80[0:CUT3, 384:512] = m80[0:CUT3, 384:512] - coef * sum_a[CHIP_ROWS:STACK_A]
    w80[CUT3:, 384:512] = m80[CUT3:, 384:512] - coef * sum_b[EDGE:STACK]
    sum_c = direct_sum(*stacks3[1])
    w80[:, 128:256] = m80[:, 128:256] - coef * sum_c[0:CHIP_ROWS]
    w80[0:CUT2, 256:384] = m80[0:CUT2, 256:384] - coef * sum_c[CHIP_ROWS:STACK_A]
    w80[CUT2:, 256:384] = m80[CUT2:, 256:384] - coef * sum_b[CHIP_ROWS:EDGE]
    pass_w = remote(w80.at[other_rows], w_in, ps_x.at[1], pr_x.at[1], partner)
    pass_w.start()
    w_roll = w80[...].astype(BF16)

    remote(emb.at[other], emb.at[other], ps_x.at[0], pr_x.at[0], partner).wait_recv()
    oy = [order_of(lax.rem(y + 4 - my_y, 4)) for y in range(4)]
    ox = [order_of(lax.rem(x + 4 - my_x, 4)) for x in range(4)]
    oz = [order_of(lax.rem(z + 4 - my_z, 4)) for z in range(4)]
    for e in range(2):
        part = tdot(emb[e], w_roll)
        for n in range(16):
            block = e * 16 + n
            y, x, z_hi = block // 8, (block // 2) % 4, block % 2
            for z_lo in range(2):
                z = z_hi * 2 + z_lo
                for h in range(2):
                    lane = (z_lo * 2 + h) * 128
                    piece = part[n * 8 : (n + 1) * 8, lane : lane + 128]
                    if h == 0:
                        t1[h, ox[x], oy[y], oz[z]] = piece
                    else:
                        t1[h, oz[z], oy[y], ox[x]] = piece
    tail = (("x", "y", "z"), ("z", "y", "x"))
    stages = ((t1b, rt1), (t2, rt2), (t3, rt3))
    tails = [
        [direct(buf.at[h], into.at[h], 6 + 2 * n + h, tail[h][n]) for h in range(2)]
        for n, (buf, into) in enumerate(stages)
    ]
    for n, (buf, into) in enumerate(stages):
        for h in range(2):
            if n == 0:
                t1b[h] = t1[h].reshape(4, 4, 2, 16, 128).astype(BF16)
            else:
                before, came = stages[n - 1]
                done = direct_sum(before.at[h], came.at[h], tails[n - 1][h])
                buf[h] = done.reshape(buf.shape[1:])
            for copy in tails[n][h]:
                copy.start()
        if n < 2:
            pl.loop(cuts[2 + n], cuts[3 + n])(attend)
    for _, _, copies in stacks2 + stacks3:
        for copy in copies:
            copy.wait_send()
    for copies in pieces:
        for copy in copies:
            copy.wait_send()
    pass_emb.wait_send()
    pass_w.wait_send()
    for q in range(2):
        w_out[:, quarter(q, core)] = w80[own_rows, q * 256 : (q + 1) * 256]
    pass_w.wait_recv()
    for q in range(2):
        w_out[:, quarter(q, other)] = w_in[:, q * 256 : (q + 1) * 256]
    for h in range(2):
        own = direct_sum(t3.at[h], rt3.at[h], tails[2][h])
        share = mix[h]
        lanes = slice(h * HD, (h + 1) * HD)
        value = (share * own + (1.0 - share) * first[:, lanes].astype(F32)).astype(BF16)
        value_out[:, lanes] = value
        fresh_value = value.astype(F32)
        for n in range(h * group, (h + 1) * group):
            att_out[:, n * HD : (n + 1) * HD] = (
                mixed[:, n, :] + fresh_prob[:, n, :] * fresh_value
            ).astype(BF16)

    for stage in tails:
        for copies in stage:
            for copy in copies:
                copy.wait_send()


def update(
    activations,
    grad_out,
    master_w,
    embed_table,
    cache_keys,
    cache_values,
    tokens,
    first_value,
    queries,
    new_key,
    mix,
    lengths,
    tokens_total,
):
    width = activations.shape[1]
    vocab = embed_table.shape[0]
    depth = activations.shape[0]
    rows = queries.shape[0]
    heads = queries.shape[1] // HD
    coef = 1.0 / math.sqrt(tokens_total * width)
    dma = pltpu.SemaphoreType.DMA
    vmem = pltpu.VMEM
    tile = (STACK, 128)
    tile_a = (STACK_A, 128)
    anywhere = pl.BlockSpec(memory_space=pl.ANY)
    whole = pl.BlockSpec(memory_space=pltpu.VMEM)
    scalars = pl.BlockSpec(memory_space=pltpu.SMEM)
    return pl.pallas_call(
        functools.partial(kernel, coef),
        out_shape=(
            vmem(master_w.shape, F32),
            vmem(first_value.shape, BF16),
            vmem(queries.shape, BF16),
        ),
        in_specs=[anywhere] * 6 + [whole] * 4 + [scalars] * 2,
        out_specs=(whole, whole, whole),
        scratch_shapes=[
            vmem((STEPS, depth, BLOCK), BF16),
            vmem((STEPS, depth, BLOCK), BF16),
            vmem((depth, 512), BF16),
            vmem((depth, 512), BF16),
            vmem((STEPS, vocab, BLOCK), BF16),
            vmem((256, vocab), BF16),
            vmem(cache_keys.shape, BF16),
            vmem(cache_values.shape, BF16),
            vmem((rows, heads, HD), F32),
            vmem((rows, 2, HD), F32),
            vmem((rows, heads, HD), F32),
            vmem((rows, heads, HD), F32),
            vmem((CHIP_ROWS, 512), F32),
            vmem((CHIP_ROWS, 512), F32),
            vmem((ROWS, 512), F32),
            vmem((STEPS, 2, 128, BLOCK), BF16),
            vmem((STEPS, 128, BLOCK), BF16),
            vmem((4, 4, 4) + tile_a, BF16),
            vmem((4, 6, 2) + tile_a, BF16),
            vmem((4, 4, 4) + tile_a, BF16),
            vmem((STEPS, 6) + tile_a, BF16),
            vmem((4, 4, 4) + tile, BF16),
            vmem((6, 2, 4) + tile, BF16),
            vmem((4, 4) + tile_a, BF16),
            vmem((4, 4) + tile_a, BF16),
            vmem((3, 4) + tile_a, BF16),
            vmem((3, 4) + tile_a, BF16),
            vmem((4, 4) + tile, BF16),
            vmem((3, 4) + tile, BF16),
            vmem((4,) + tile_a, BF16),
            vmem((4,) + tile_a, BF16),
            vmem((3,) + tile_a, BF16),
            vmem((3,) + tile_a, BF16),
            vmem((4,) + tile, BF16),
            vmem((3,) + tile, BF16),
            vmem((2, CHIP_ROWS, 128), BF16),
            vmem((2, 4, 4, 4, 8, 128), F32),
            vmem((2, 4, 4, 2, 16, 128), BF16),
            vmem((2, 3, 4, 2, 16, 128), BF16),
            vmem((2, 4, 4, 8, 128), F32),
            vmem((2, 3, 4, 8, 128), F32),
            vmem((2, 4, 8, 128), F32),
            vmem((2, 3, 8, 128), F32),
            dma((STEPS,)),
            dma((STEPS,)),
            dma((4,)),
            dma((2,)),
            dma((STEPS,)),
            dma((STEPS,)),
            dma((4,)),
            dma((4,)),
            dma((STEPS,)),
            dma((STEPS,)),
            dma((2,)),
            dma((2,)),
            dma((4, 6)),
            dma((4, 6)),
            dma((STEPS, 6)),
            dma((STEPS, 6)),
            dma((6,)),
            dma((6,)),
            dma((4, 3)),
            dma((4, 3)),
            dma((12, 3)),
            dma((12, 3)),
        ],
        compiler_params=pltpu.CompilerParams(
            collective_id=0, has_side_effects=True, vmem_limit_bytes=60 * 1024 * 1024
        ),
        cost_estimate=pl.CostEstimate(
            flops=2 * depth * width * 1024 + 2 * vocab * width * 256,
            bytes_accessed=2 * width * (depth + vocab),
            transcendentals=0,
        ),
        name="update",
    )(
        activations,
        grad_out,
        master_w,
        embed_table,
        cache_keys,
        cache_values,
        tokens,
        first_value,
        queries,
        new_key,
        mix,
        lengths,
    )


def per_device(
    activations,
    grad_out,
    master_w,
    embed_table,
    token_ids,
    queries,
    cache_keys,
    cache_values,
    new_key,
    first_value,
    residual_mix,
    lengths,
):
    devices_all = lax.axis_size("fsdp") * lax.axis_size("tp")
    return update(
        activations,
        grad_out,
        master_w,
        embed_table,
        cache_keys,
        cache_values,
        token_ids.reshape(1, -1),
        first_value,
        queries,
        new_key,
        residual_mix,
        lengths,
        activations.shape[0] * devices_all,
    )


def solution(mesh):
    return jax.shard_map(
        per_device,
        mesh=mesh,
        in_specs=(
            P(("fsdp", "tp"), None),
            P(("fsdp", "tp"), None),
            P(("fsdp", "tp"), None),
            P(("fsdp", "tp"), None),
            P(),
            P("fsdp", "tp"),
            P("fsdp", None, "tp"),
            P("fsdp", None, "tp"),
            P("fsdp", "tp"),
            P("fsdp", "tp"),
            P("tp"),
            P("fsdp"),
        ),
        out_specs=(P(("fsdp", "tp"), None), P("fsdp", "tp"), P("fsdp", "tp")),
        check_vma=False,
    )
```
